256 devices in a mesh: scen: 8 (over z), blk: 32 (over x, y, core).
Axes of the slice: x: 4, y: 4, z: 8, core: 2. Of those that a mesh axis runs over, the one named last changes fastest.
Arguments:
- local_tiles: bfloat16 [7168, 128, 128], P('blk'), may hold values from -0.1875 to 0.1875
- local_rows: int32 [7168], P('blk'), may hold values from 0 to 39
- local_cols: int32 [7168], P('blk'), may hold values from 0 to 31
- far_tiles: bfloat16 [1024, 1, 128, 128], P('blk'), may hold values from -0.375 to 0.375
- far_rows: int32 [1024, 1], P('blk'), may hold values from 0 to 39
- far_cols: int32 [1024, 1], P('blk'), may hold values from 0 to 31
- link_tiles: bfloat16 [4096, 128, 128], P(('scen', 'blk')), may hold values from -0.5 to 0.5
- link_rows: int32 [4096], P(('scen', 'blk')), may hold values from 0 to 39
- link_cols: int32 [4096], P(('scen', 'blk')), may hold values from 0 to 15
- inflows: bfloat16 [256, 163840], P('scen', 'blk'), may hold values from -6 to 6
- recourse_cost: float32 [131072], P('blk'), may hold values from -6 to 6
- first_cost: float32 [2048], P('scen'), may hold values from -6 to 6
- first_section: float32 [2048], P('scen'), may hold values from 0 to 2
- recourse: float32 [256, 131072], P('scen', 'blk'), may hold values from 0 to 2
- duals: float32 [256, 163840], P('scen', 'blk'), may hold values from -6 to 6
Outputs:
- first_out: float32 [2048], P('scen')
- recourse_out: float32 [256, 131072], P('scen', 'blk')
- duals_out: float32 [256, 163840], P('scen', 'blk')
The draws below stay inside these ranges and needn't reach their ends.
Inputs may be any that keep to these rules, and one draw needn't show every extreme that they name: `far_cols`: far tile entry (b * (blk size) + p, k) lies in a row block owned by blk index b and in a column block owned by blk index p; every blk index holds exactly 1 far tiles for every blk index, its own included. `far_rows`: row offsets count within the row blocks of the holding blk index. Linking tiles of device (g, b) lie in row blocks owned by b; link_cols names a block of 128 first-section columns.
All inputs are finite; a program needn't handle non-finite values.
Results may differ from the reference program's by a relative error of at most 0.017.
Values may be sent and summed in bfloat16 or wider, within the bound.
A program may use at most 64 MiB of HBM per device.

```python
import jax
import jax.numpy as jnp
from jax import lax

TILE = 128
S_G = 32
RB_DEV = 40
CB_DEV = 32
TL_DEV = 224
CAP = 1
LINK_DEV = 16
XB_DEV = 2
ITERS = 2
SCEN = 256
ROWS = 163840
COLS = 131072
XCOLS = 2048
N_SCEN = 8
N_BLK = 32


def touch_ends(entries, key, smallest, top_value):
    longest = entries.shape.index(max(entries.shape))
    spots = []
    for shift in (0, 1):
        where = [jax.random.randint(jax.random.fold_in(key, axis), (), 0, length) for axis, length in enumerate(entries.shape)]
        where[longest] = (where[longest] + shift) % entries.shape[longest]
        spots.append(tuple(where))
    return entries.at[spots[0]].set(smallest).at[spots[1]].set(top_value)


def steps_of(stream_key, shape, cuts, least, largest):
    loudness = 1.0
    for dim, blocks in cuts:
        draws = jax.random.uniform(jax.random.fold_in(jax.random.fold_in(stream_key, 6), dim), (blocks,), jnp.float32, least / len(cuts), largest / len(cuts))
        loudness = loudness * jnp.repeat(jnp.exp(draws), shape[dim] // blocks).reshape((-1,) + (1,) * (len(shape) - 1 - dim))
    return loudness


def centred(own_key, dims, deviation, limit, pieces=(), kind=jnp.bfloat16):
    result = deviation * jax.random.normal(own_key, dims, jnp.float32)
    if pieces:
        result = result * steps_of(own_key, dims, pieces, -0.22, 0.18)
    return jnp.clip(result, -limit, limit).astype(kind)


def setup_inputs(seed: int = 0) -> dict:
    key_list = jax.random.split(jax.random.key(seed), 16)
    return {
        "local_tiles": centred(key_list[0], (N_BLK * TL_DEV, TILE, TILE), (TILE * (TL_DEV + 4 * N_BLK * CAP) // RB_DEV) ** -0.5, 0.1875, ((0, 32),)),
        "local_rows": touch_ends(jax.random.randint(key_list[1], (N_BLK * TL_DEV,), 0, RB_DEV), jax.random.fold_in(key_list[1], 1), 0, RB_DEV - 1).astype(jnp.int32),
        "local_cols": touch_ends(jax.random.randint(key_list[2], (N_BLK * TL_DEV,), 0, CB_DEV), jax.random.fold_in(key_list[2], 1), 0, CB_DEV - 1).astype(jnp.int32),
        "far_tiles": centred(key_list[3], (N_BLK * N_BLK, CAP, TILE, TILE), (TILE * (TL_DEV + 4 * N_BLK * CAP) // (4 * RB_DEV)) ** -0.5, 0.375, ((0, 32),)),
        "far_rows": touch_ends(jax.random.randint(key_list[4], (N_BLK * N_BLK, CAP), 0, RB_DEV), jax.random.fold_in(key_list[4], 1), 0, RB_DEV - 1).astype(jnp.int32),
        "far_cols": touch_ends(jax.random.randint(key_list[5], (N_BLK * N_BLK, CAP), 0, CB_DEV), jax.random.fold_in(key_list[5], 1), 0, CB_DEV - 1).astype(jnp.int32),
        "link_tiles": centred(key_list[6], (N_SCEN * N_BLK * LINK_DEV, TILE, TILE), (max(9 * TILE * LINK_DEV * N_BLK // (XB_DEV * S_G * N_SCEN * N_SCEN), 1)) ** -0.5, 0.5, ((0, 256),)),
        "link_rows": touch_ends(jax.random.randint(key_list[7], (N_SCEN * N_BLK * LINK_DEV,), 0, RB_DEV), jax.random.fold_in(key_list[7], 1), 0, RB_DEV - 1).astype(jnp.int32),
        "link_cols": touch_ends(jax.random.randint(key_list[8], (N_SCEN * N_BLK * LINK_DEV,), 0, XB_DEV * N_SCEN), jax.random.fold_in(key_list[8], 1), 0, (XB_DEV * N_SCEN) - 1).astype(jnp.int32),
        "inflows": centred(key_list[9], (SCEN, ROWS), 1.0, 6.0, ((0, 8), (1, 32))),
        "recourse_cost": centred(key_list[10], (COLS,), 1.0, 6.0, ((0, 32),), jnp.float32),
        "first_cost": centred(key_list[11], (XCOLS,), 1.0, 6.0, ((0, 8),), jnp.float32),
        "first_section": jnp.clip(2.0 * jax.random.uniform(key_list[12], (XCOLS,), jnp.float32) ** steps_of(key_list[12], (XCOLS,), ((0, 8),), -0.2, 0.2), 0.0, 2.0),
        "recourse": jnp.clip(2.0 * jax.random.uniform(key_list[13], (SCEN, COLS), jnp.float32) ** steps_of(key_list[13], (SCEN, COLS), ((0, 8), (1, 32)), -0.2, 0.2), 0.0, 2.0),
        "duals": centred(key_list[14], (SCEN, ROWS), 1.0, 6.0, ((0, 8), (1, 32)), jnp.float32),
    }


primal_stepsize = 0.4
first_step = 2.0
dual_step = 0.4


def recourse_listing(local_rows, local_cols, far_rows, far_cols):
    owner = jnp.arange(N_BLK * TL_DEV, dtype=jnp.int32) // TL_DEV
    pair = jnp.arange(N_BLK * N_BLK, dtype=jnp.int32)
    holder = jnp.broadcast_to((pair // N_BLK)[:, None], (N_BLK * N_BLK, CAP))
    peer = jnp.broadcast_to((pair % N_BLK)[:, None], (N_BLK * N_BLK, CAP))
    row_ids = jnp.concatenate([owner * RB_DEV + local_rows, (holder * RB_DEV + far_rows).reshape(-1)])
    column_ids = jnp.concatenate([owner * CB_DEV + local_cols, (peer * CB_DEV + far_cols).reshape(-1)])
    return row_ids.astype(jnp.int32), column_ids.astype(jnp.int32)


def to_half(values):
    rounded = lax.optimization_barrier(values.astype(jnp.bfloat16))
    return rounded.astype(jnp.float32)


def reference(local_tiles, local_rows, local_cols, far_tiles, far_rows, far_cols, link_tiles, link_rows, link_cols, inflows, recourse_cost, first_cost, first_section, recourse, duals):
    row_total = RB_DEV * N_BLK
    col_total = CB_DEV * N_BLK
    first_total = XB_DEV * N_SCEN
    row_ids, column_ids = recourse_listing(local_rows, local_cols, far_rows, far_cols)
    all_tiles = jnp.concatenate([local_tiles.reshape(-1, TILE, TILE), far_tiles.reshape(-1, TILE, TILE)]).astype(jnp.float32)
    link_index = jnp.arange(N_SCEN * N_BLK * LINK_DEV, dtype=jnp.int32)
    link_global = ((link_index // LINK_DEV) % N_BLK) * RB_DEV + link_rows
    group_rows = link_global.astype(jnp.int32).reshape(N_SCEN, -1)
    group_cols = link_cols.reshape(N_SCEN, -1)
    group_tiles = link_tiles.astype(jnp.float32).reshape(N_SCEN, -1, TILE, TILE)

    def primal_group(items):
        dual_group, rows_here, cols_here, tiles_here = items
        half = to_half(dual_group).reshape(S_G, row_total, TILE)
        picked = jnp.take(half, row_ids, axis=1)
        terms = jnp.einsum("snr,nrc->nsc", picked, all_tiles)
        gradient = jax.ops.segment_sum(terms, column_ids, num_segments=col_total)
        gradient = jnp.transpose(gradient, (1, 0, 2)).reshape(S_G, -1)
        link_pick = jnp.take(half, rows_here, axis=1)
        link_terms = jnp.einsum("snr,nrc->nc", link_pick, tiles_here)
        first_part = jax.ops.segment_sum(link_terms, cols_here, num_segments=first_total)
        return gradient, first_part

    first_now = first_section
    recourse_now = recourse
    duals_now = duals
    for step in range(ITERS):
        gradient, first_parts = lax.map(primal_group, (duals_now.reshape(N_SCEN, S_G, -1), group_rows, group_cols, group_tiles))
        recourse_gradient = gradient.reshape(SCEN, -1)
        first_grad = jnp.sum(first_parts, axis=0).reshape(-1)
        first_new = jnp.maximum(first_now - first_step * (first_cost - first_grad / SCEN), 0.0)
        recourse_new = jnp.maximum(recourse_now - primal_stepsize * (recourse_cost[None, :] - recourse_gradient), 0.0)
        first_bar = to_half(2.0 * first_new - first_now).reshape(first_total, TILE)
        recourse_bar = to_half(2.0 * recourse_new - recourse_now)

        def dual_group(items):
            bar_group, rows_here, cols_here, tiles_here = items
            blocks = bar_group.reshape(S_G, col_total, TILE)
            picked = jnp.take(blocks, column_ids, axis=1)
            terms = jnp.einsum("snc,nrc->nsr", picked, all_tiles)
            matrix_image = jax.ops.segment_sum(terms, row_ids, num_segments=row_total)
            matrix_image = jnp.transpose(matrix_image, (1, 0, 2))
            link_pick = jnp.take(first_bar, cols_here, axis=0)
            link_terms = jnp.einsum("nc,nrc->nr", link_pick, tiles_here)
            link_image = jax.ops.segment_sum(link_terms, rows_here, num_segments=row_total)
            return (matrix_image + link_image[None]).reshape(S_G, -1)

        matrix_image = lax.map(dual_group, (recourse_bar.reshape(N_SCEN, S_G, -1), group_rows, group_cols, group_tiles)).reshape(SCEN, -1)
        duals_now = duals_now + dual_step * (inflows.astype(jnp.float32) - matrix_image)
        first_now = first_new
        recourse_now = recourse_new
    return first_now, recourse_now, duals_now
```

```python
import functools

import jax
import jax.numpy as jnp
from jax import lax
from jax.experimental import pallas as pl
from jax.experimental.pallas import tpu as pltpu
from jax.sharding import PartitionSpec as P

TILE = 128
ITERS = 2
S = 32
RB = 40
CB = 32
NL = 224
NF = 32
NK = 16
XB = 2
NS = 8
NB = 32
FB = XB * NS
W = 256
WF = 128
SPLIT = 128

PRIMAL = 0.4
FIRST = 2.0
DUAL = 0.4
LIMITS = (NL - 1, RB - 1, 1, NL, NL - 1, CB - 1, 1, NL)
FAR_LIMITS = (NF - 1, CB - 1, 1, NF)
MESH = pl.DeviceIdType.MESH
F32 = jnp.float32
BF16 = jnp.bfloat16


def dot(a, b):
    return jnp.dot(a, b, preferred_element_type=F32)


def dot_t(a, b):
    return lax.dot_general(a, b, (((1,), (1,)), ((), ())), preferred_element_type=F32)


def whole(value, top):
    return jnp.clip(value[0:1].astype(jnp.int32), 0, top)


def sorted_tables(key, other, count, width, empty):
    rows = lax.broadcasted_iota(jnp.int32, (width, width), 0).astype(F32)
    lanes = lax.broadcasted_iota(jnp.int32, (width, width), 1).astype(F32)
    key_j = jnp.broadcast_to(key[0:1], (width, width))
    key_i = key_j.T
    before = (key_j * W + lanes) < (key_i * W + rows)
    rank = dot(before.astype(F32).astype(BF16), jnp.ones((width, width), BF16))
    place = (rank == lanes).astype(F32).astype(BF16)
    lane8 = lax.broadcasted_iota(jnp.int32, (8, width), 1).astype(F32)
    source = jnp.concatenate([lane8, other, key, key], axis=0).astype(BF16)
    moved = dot(source, place)
    order, other_sorted, key_sorted = moved[0:8], moved[8:16], moved[16:24]
    previous = pltpu.roll(key_sorted, 1, 1)
    keep = ((key_sorted == previous) & (lane8 > 0)).astype(F32)
    ones = jnp.ones((16, width), BF16)
    upto = dot(ones, (key_i <= lanes).astype(F32).astype(BF16))[0:8]
    under = dot(ones, (key_i < lanes).astype(F32).astype(BF16))[0:8]
    last = jnp.where(upto > under, upto - 1.0, float(empty))
    return order, other_sorted, keep, last


def kernel(
    far_rows_s,
    far_cols_s,
    link_rows_s,
    link_cols_s,
    local_rows_v,
    local_cols_v,
    far_rows_v,
    cost_v,
    first_cost_v,
    first_v,
    local_hbm,
    far_hbm,
    link_hbm,
    inflow_hbm,
    rec_hbm,
    dual_hbm,
    first_out,
    rec_out,
    dual_out,
    tiles,
    far,
    link,
    inflow,
    half,
    hsum,
    bars,
    run,
    run_far,
    run_want,
    link_lhs,
    link_img,
    table_v,
    table_far_v,
    table_want_v,
    table,
    table_far,
    table_want,
    idx_send,
    idx_recv,
    term_send,
    term_recv,
    col_send,
    col_recv,
    z_send,
    z_recv,
    b_send,
    b_recv,
    bar_recv,
    load_sem,
    idx_sem,
    sems,
):
    me_s = lax.axis_index("scen")
    me_b = lax.axis_index("blk")
    mx, my, mc = me_b // 8, (me_b // 2) % 4, me_b % 2

    def peer(k):
        j = ((k + 1) * 13) % 32
        jx, jy, jc = j // 8, (j // 2) % 4, j % 2
        return (((mx + jx) % 4) * 4 + (my + jy) % 4) * 2 + (mc + jc) % 2

    def z_peer(k):
        return (me_s + k) % NS

    barrier = pltpu.get_barrier_semaphore()

    def greet(k, c):
        pl.semaphore_signal(barrier, inc=1, device_id=(me_s, peer(k)), device_id_type=MESH)
        return c

    lax.fori_loop(0, NB - 1, greet, 0)

    def greet_z(k, c):
        pl.semaphore_signal(barrier, inc=1, device_id=(z_peer(k), me_b), device_id_type=MESH)
        return c

    lax.fori_loop(1, NS, greet_z, 0)

    loads = [
        pltpu.make_async_copy(dual_hbm, dual_out, load_sem.at[0]),
        pltpu.make_async_copy(far_hbm, far, load_sem.at[1]),
        pltpu.make_async_copy(link_hbm, link, load_sem.at[2]),
        pltpu.make_async_copy(local_hbm, tiles, load_sem.at[3]),
        pltpu.make_async_copy(rec_hbm, rec_out, load_sem.at[4]),
        pltpu.make_async_copy(inflow_hbm, inflow, load_sem.at[5]),
    ]
    for load in loads:
        load.start()

    for p in range(NB):
        idx_send[p] = jnp.full((8, TILE), far_cols_s[p], jnp.int32)

    pad = jnp.full((8, W - NL), 64.0, F32)
    row_key = jnp.concatenate(
        [jnp.broadcast_to(local_rows_v[...].astype(F32), (8, NL)), pad], axis=1
    )
    col_key = jnp.concatenate(
        [jnp.broadcast_to(local_cols_v[...].astype(F32), (8, NL)), pad], axis=1
    )
    pad_far = jnp.full((8, WF - NF), 64.0, F32)
    far_key = jnp.concatenate(
        [jnp.broadcast_to(far_rows_v[...].astype(F32), (8, NF)), pad_far], axis=1
    )
    col_tables = sorted_tables(col_key, row_key, NL, W, NL)
    row_tables = sorted_tables(row_key, col_key, NL, W, NL)
    for i, value in enumerate(col_tables + row_tables):
        table_v[i : i + 1, :] = whole(value, LIMITS[i])
    far_tables = sorted_tables(far_key, far_key, NF, WF, NF)
    for i, value in enumerate(far_tables):
        table_far_v[i : i + 1, :] = whole(value, FAR_LIMITS[i])
    to_smem = [
        pltpu.make_async_copy(table_v, table, load_sem.at[6]),
        pltpu.make_async_copy(table_far_v, table_far, load_sem.at[7]),
    ]
    for copy in to_smem:
        copy.start()
    zero = jnp.zeros((S, TILE), F32)
    run[NL] = zero
    run_far[NF] = zero
    run_want[NF] = zero

    loads[0].wait()

    def to_half(rb, c):
        value = dual_out[:, pl.ds(pl.multiple_of(rb * TILE, TILE), TILE)].astype(BF16)
        half[rb] = value
        hsum[pl.ds(rb, 1), :] = jnp.sum(value.astype(F32), axis=0, keepdims=True)
        return c

    lax.fori_loop(0, RB, to_half, 0, unroll=8)
    loads[1].wait()

    for it in range(ITERS):
        def send_index(k, c):
            p = peer(k)
            pltpu.make_async_remote_copy(
                src_ref=idx_send.at[p],
                dst_ref=idx_recv.at[me_b],
                send_sem=idx_sem.at[0],
                recv_sem=idx_sem.at[1],
                device_id=(me_s, p),
                device_id_type=MESH,
            ).start()
            return c

        def far_term(k, c):
            p = peer(k)
            term_send[it, p] = dot(half[far_rows_s[p]], far[p]).astype(BF16)
            return c

        def send_term(k, c):
            p = peer(k)
            pltpu.make_async_remote_copy(
                src_ref=term_send.at[it, p],
                dst_ref=term_recv.at[it, me_b],
                send_sem=sems.at[it, 0, 0],
                recv_sem=sems.at[it, 0, 1],
                device_id=(me_s, p),
                device_id_type=MESH,
            ).start()
            return c

        for g in range(0, NB, 16):
            lax.fori_loop(g, g + 16, far_term, 0, unroll=16)
            if it == 0 and g == 0:
                pl.semaphore_wait(barrier, NB - 1 + NS - 1)
            lax.fori_loop(g, min(g + 16, NB - 1), send_term, 0)
        if it == 0:
            lax.fori_loop(0, NB - 1, send_index, 0)
        term_recv[it, me_b] = term_send[it, me_b]

        if it == 0:
            loads[2].wait()
        for n in range(NK):
            link_lhs[n : n + 1, :] = hsum[pl.ds(link_rows_s[n], 1), :]
        sums = link_lhs[...]
        high = sums.astype(BF16)
        low = (sums - high.astype(F32)).astype(BF16)
        lhs = jnp.concatenate([high, low], axis=0)
        block = lax.broadcasted_iota(jnp.int32, (FB, TILE), 0)
        part = jnp.zeros((FB, TILE), F32)
        for n in range(NK):
            product = dot(lhs, link[n])
            row = product[n : n + 1] + product[NK + n : NK + n + 1]
            part = part + jnp.where(block == link_cols_s[n], row, 0.0)
        for g in range(NS):
            z_send[it, g] = part[g * XB : (g + 1) * XB]

        def send_z(k, c):
            s = z_peer(k)
            pltpu.make_async_remote_copy(
                src_ref=z_send.at[it, s],
                dst_ref=z_recv.at[it, me_s],
                send_sem=sems.at[it, 1, 0],
                recv_sem=sems.at[it, 1, 1],
                device_id=(s, me_b),
                device_id_type=MESH,
            ).start()
            return c

        lax.fori_loop(1, NS, send_z, 0)
        z_recv[it, me_s] = z_send[it, me_s]

        if it == 0:
            for copy in to_smem:
                copy.wait()
            loads[3].wait()

        def gradient_step(n, total):
            keep = table[2, n].astype(F32)
            total = total * keep + dot(half[table[1, n]], tiles[table[0, n]])
            run[n] = total
            return total

        total = lax.fori_loop(0, SPLIT, gradient_step, zero, unroll=32)

        pltpu.make_async_copy(
            z_recv.at[it, pl.ds(0, NS - 1)], z_recv.at[it, pl.ds(0, NS - 1)], sems.at[it, 1, 1]
        ).wait()
        b_send[it] = jnp.sum(z_recv[it], axis=0)

        def send_b(k, c):
            pltpu.make_async_remote_copy(
                src_ref=b_send.at[it],
                dst_ref=b_recv.at[it, me_b],
                send_sem=sems.at[it, 2, 0],
                recv_sem=sems.at[it, 2, 1],
                device_id=(me_s, peer(k)),
                device_id_type=MESH,
            ).start()
            return c

        lax.fori_loop(0, NB - 1, send_b, 0)
        b_recv[it, me_b] = b_send[it]
        lax.fori_loop(SPLIT, NL, gradient_step, total, unroll=32)

        if it == 0:
            pltpu.make_async_copy(
                idx_recv.at[pl.ds(0, NB - 1)], idx_recv.at[pl.ds(0, NB - 1)], idx_sem.at[1]
            ).wait()
            idx_recv[me_b] = idx_send[me_b]
            lane = lax.broadcasted_iota(jnp.int32, (8, WF), 1)
            wanted = jnp.full((8, WF), 64, jnp.int32)
            for q in range(NB):
                wanted = jnp.where(lane == q, idx_recv[q], wanted)
            wanted = wanted.astype(F32)
            want_tables = sorted_tables(wanted, wanted, NF, WF, NF)
            for i, value in enumerate((want_tables[0], wanted) + want_tables[2:]):
                table_want_v[i : i + 1, :] = whole(value, FAR_LIMITS[i])
            want_copy = pltpu.make_async_copy(table_want_v, table_want, load_sem.at[6])
            want_copy.start()
            want_copy.wait()
            loads[4].wait()

        pltpu.make_async_copy(
            term_recv.at[it, pl.ds(0, NB - 1)],
            term_recv.at[it, pl.ds(0, NB - 1)],
            sems.at[it, 0, 1],
        ).wait()

        def want_step(k, total):
            keep = table_want[2, k].astype(F32)
            total = total * keep + term_recv[it, table_want[0, k]].astype(F32)
            run_want[k] = total
            return total

        lax.fori_loop(0, NF, want_step, zero, unroll=8)

        def update_recourse(cb, c):
            at = pl.ds(pl.multiple_of(cb * TILE, TILE), TILE)
            grad = run[table[3, cb]] + run_want[table_want[3, cb]]
            old = rec_out[:, at]
            new = jnp.maximum(old - PRIMAL * (cost_v[:, at] - grad), 0.0)
            bars[cb] = (2.0 * new - old).astype(BF16)
            rec_out[:, at] = new
            return c

        lax.fori_loop(0, CB, update_recourse, 0, unroll=8)

        def gather_col(k, c):
            p = peer(k)
            col_send[it, p] = bars[table_want[1, p]]
            return c

        def send_col(k, c):
            p = peer(k)
            pltpu.make_async_remote_copy(
                src_ref=col_send.at[it, p],
                dst_ref=col_recv.at[it, me_b],
                send_sem=sems.at[it, 3, 0],
                recv_sem=sems.at[it, 3, 1],
                device_id=(me_s, p),
                device_id_type=MESH,
            ).start()
            return c

        lax.fori_loop(0, NB, gather_col, 0, unroll=8)
        lax.fori_loop(0, NB - 1, send_col, 0)
        col_recv[it, me_b] = col_send[it, me_b]

        pltpu.make_async_copy(
            b_recv.at[it, pl.ds(0, NB - 1)], b_recv.at[it, pl.ds(0, NB - 1)], sems.at[it, 2, 1]
        ).wait()
        first_grad = jnp.sum(b_recv[it], axis=0)
        old_first = first_v[...] if it == 0 else first_out[...]
        new_first = jnp.maximum(
            old_first - FIRST * (first_cost_v[...] - first_grad / (S * NS)), 0.0
        )
        first_out[...] = new_first
        bar_recv[it, me_s] = (2.0 * new_first - old_first).astype(BF16).astype(F32)

        def send_bar(k, c):
            pltpu.make_async_remote_copy(
                src_ref=bar_recv.at[it, me_s],
                dst_ref=bar_recv.at[it, me_s],
                send_sem=sems.at[it, 4, 0],
                recv_sem=sems.at[it, 4, 1],
                device_id=(z_peer(k), me_b),
                device_id_type=MESH,
            ).start()
            return c

        lax.fori_loop(1, NS, send_bar, 0)

        def image_step(n, total):
            keep = table[6, n].astype(F32)
            total = total * keep + dot_t(bars[table[5, n]], tiles[table[4, n]])
            run[n] = total
            return total

        lax.fori_loop(0, NL, image_step, zero, unroll=32)

        pltpu.make_async_copy(
            bar_recv.at[it, pl.ds(0, NS - 1)], bar_recv.at[it, pl.ds(0, NS - 1)], sems.at[it, 4, 1]
        ).wait()
        for n in range(NK):
            b = link_cols_s[n]
            link_lhs[n : n + 1, :] = bar_recv[it, b // XB, pl.ds(b % XB, 1), :]
        lhs = link_lhs[...].astype(BF16)
        block = lax.broadcasted_iota(jnp.int32, (RB, TILE), 0)
        image = jnp.zeros((RB, TILE), F32)
        for n in range(NK):
            row = dot_t(lhs, link[n])[n : n + 1]
            image = image + jnp.where(block == link_rows_s[n], row, 0.0)
        link_img[...] = image

        pltpu.make_async_copy(
            col_recv.at[it, pl.ds(0, NB - 1)],
            col_recv.at[it, pl.ds(0, NB - 1)],
            sems.at[it, 3, 1],
        ).wait()

        def far_step(k, total):
            q = table_far[0, k]
            keep = table_far[2, k].astype(F32)
            total = total * keep + dot_t(col_recv[it, q], far[q])
            run_far[k] = total
            return total

        lax.fori_loop(0, NF, far_step, zero, unroll=32)
        if it == 0:
            loads[5].wait()

        def update_duals(rb, c):
            at = pl.ds(pl.multiple_of(rb * TILE, TILE), TILE)
            image = run[table[7, rb]] + run_far[table_far[3, rb]] + link_img[pl.ds(rb, 1), :]
            new = dual_out[:, at] + DUAL * (inflow[:, at].astype(F32) - image)
            dual_out[:, at] = new
            if it < ITERS - 1:
                value = new.astype(BF16)
                half[rb] = value
                hsum[pl.ds(rb, 1), :] = jnp.sum(value.astype(F32), axis=0, keepdims=True)
            return c

        lax.fori_loop(0, RB, update_duals, 0, unroll=8)

    def sent(buffer, sem):
        pltpu.make_async_copy(buffer, buffer, sem).wait()

    sent(idx_recv.at[pl.ds(0, NB - 1)], idx_sem.at[0])
    for it in range(ITERS):
        sent(term_recv.at[it, pl.ds(0, NB - 1)], sems.at[it, 0, 0])
        sent(z_recv.at[it, pl.ds(0, NS - 1)], sems.at[it, 1, 0])
        sent(b_recv.at[it, pl.ds(0, NB - 1)], sems.at[it, 2, 0])
        sent(col_recv.at[it, pl.ds(0, NB - 1)], sems.at[it, 3, 0])
        sent(bar_recv.at[it, pl.ds(0, NS - 1)], sems.at[it, 4, 0])


def body(
    local_tiles,
    local_rows,
    local_cols,
    far_tiles,
    far_rows,
    far_cols,
    link_tiles,
    link_rows,
    link_cols,
    inflows,
    recourse_cost,
    first_cost,
    first_section,
    recourse,
    duals,
):
    smem = pl.BlockSpec(memory_space=pltpu.SMEM)
    vmem = pl.BlockSpec(memory_space=pltpu.VMEM)
    hbm = pl.BlockSpec(memory_space=pl.ANY)
    dma = pltpu.SemaphoreType.DMA
    first_out, rec_out, dual_out = pl.pallas_call(
        kernel,
        out_shape=(
            jax.ShapeDtypeStruct((XB, TILE), F32),
            jax.ShapeDtypeStruct((S, CB * TILE), F32),
            jax.ShapeDtypeStruct((S, RB * TILE), F32),
        ),
        in_specs=[smem] * 4 + [vmem] * 6 + [hbm] * 6,
        out_specs=(vmem, vmem, vmem),
        scratch_shapes=[
            pltpu.VMEM((NL, TILE, TILE), BF16),
            pltpu.VMEM((NF, TILE, TILE), BF16),
            pltpu.VMEM((NK, TILE, TILE), BF16),
            pltpu.VMEM((S, RB * TILE), BF16),
            pltpu.VMEM((RB, S, TILE), BF16),
            pltpu.VMEM((RB, TILE), F32),
            pltpu.VMEM((CB, S, TILE), BF16),
            pltpu.VMEM((NL + 1, S, TILE), F32),
            pltpu.VMEM((NF + 1, S, TILE), F32),
            pltpu.VMEM((NF + 1, S, TILE), F32),
            pltpu.VMEM((NK, TILE), F32),
            pltpu.VMEM((RB, TILE), F32),
            pltpu.VMEM((8, W), jnp.int32),
            pltpu.VMEM((4, WF), jnp.int32),
            pltpu.VMEM((4, WF), jnp.int32),
            pltpu.SMEM((8, W), jnp.int32),
            pltpu.SMEM((4, WF), jnp.int32),
            pltpu.SMEM((4, WF), jnp.int32),
            pltpu.VMEM((NB, 8, TILE), jnp.int32),
            pltpu.VMEM((NB, 8, TILE), jnp.int32),
            pltpu.VMEM((ITERS, NB, S, TILE), BF16),
            pltpu.VMEM((ITERS, NB, S, TILE), BF16),
            pltpu.VMEM((ITERS, NB, S, TILE), BF16),
            pltpu.VMEM((ITERS, NB, S, TILE), BF16),
            pltpu.VMEM((ITERS, NS, XB, TILE), F32),
            pltpu.VMEM((ITERS, NS, XB, TILE), F32),
            pltpu.VMEM((ITERS, XB, TILE), F32),
            pltpu.VMEM((ITERS, NB, XB, TILE), F32),
            pltpu.VMEM((ITERS, NS, XB, TILE), F32),
            dma((8,)),
            dma((2,)),
            dma((ITERS, 5, 2)),
        ],
        compiler_params=pltpu.CompilerParams(
            collective_id=0, has_side_effects=True, vmem_limit_bytes=48 << 20
        ),
        name="dispatch",
    )(
        far_rows.reshape(NF),
        far_cols.reshape(NF),
        link_rows,
        link_cols,
        local_rows.reshape(1, NL),
        local_cols.reshape(1, NL),
        far_rows.reshape(1, NF),
        recourse_cost.reshape(1, CB * TILE),
        first_cost.reshape(XB, TILE),
        first_section.reshape(XB, TILE),
        local_tiles,
        far_tiles.reshape(NF, TILE, TILE),
        link_tiles,
        inflows,
        recourse,
        duals,
    )
    return first_out.reshape(XB * TILE), rec_out, dual_out


def solution(mesh):
    in_specs = (
        P("blk", None, None),
        P("blk"),
        P("blk"),
        P("blk", None, None, None),
        P("blk", None),
        P("blk", None),
        P(("scen", "blk"), None, None),
        P(("scen", "blk")),
        P(("scen", "blk")),
        P("scen", "blk"),
        P("blk"),
        P("scen"),
        P("scen"),
        P("scen", "blk"),
        P("scen", "blk"),
    )
    out_specs = (P("scen"), P("scen", "blk"), P("scen", "blk"))
    return jax.shard_map(body, mesh=mesh, in_specs=in_specs, out_specs=out_specs, check_vma=False)
```

```python
import functools

import jax
import jax.numpy as jnp
from jax import lax
from jax.experimental import pallas as pl
from jax.experimental.pallas import tpu as pltpu
from jax.sharding import PartitionSpec as P

TILE = 128
ITERS = 2
S = 32
RB = 40
CB = 32
NL = 224
NF = 32
NK = 16
XB = 2
NS = 8
NB = 32
FB = XB * NS
W = 256
WF = 128
STEPS = sorted(
    ((a, b) for a in range(4) for b in range(4)),
    key=lambda d: -(min(d[0], 4 - d[0]) + min(d[1], 4 - d[1])),
)
ORDER = [(a, b, c) for c in (1, 0) for a, b in STEPS]
GROUPS = tuple(
    tuple(i for i in range(NB - 1) if i % 16 in part)
    for part in (range(0, 5), range(5, 11), range(11, 16))
)
UNROLL = 56

PRIMAL = 0.4
FIRST = 2.0
DUAL = 0.4
LIMITS = (NL - 1, RB - 1, 1, NL, NL - 1, CB - 1, 1, NL)
FAR_LIMITS = (NF - 1, CB - 1, 1, NF)
MESH = pl.DeviceIdType.MESH
F32 = jnp.float32
BF16 = jnp.bfloat16


def dot(a, b):
    return jnp.dot(a, b, preferred_element_type=F32)


def dot_t(a, b):
    return lax.dot_general(a, b, (((1,), (1,)), ((), ())), preferred_element_type=F32)


def whole(value, top):
    return jnp.clip(value[0:1].astype(jnp.int32), 0, top)


def sorted_tables(key, other, count, width, empty):
    rows = lax.broadcasted_iota(jnp.int32, (width, width), 0).astype(F32)
    lanes = lax.broadcasted_iota(jnp.int32, (width, width), 1).astype(F32)
    key_j = jnp.broadcast_to(key[0:1], (width, width))
    key_i = key_j.T
    before = (key_j * W + lanes) < (key_i * W + rows)
    rank = dot(before.astype(F32).astype(BF16), jnp.ones((width, width), BF16))
    place = (rank == lanes).astype(F32).astype(BF16)
    lane8 = lax.broadcasted_iota(jnp.int32, (8, width), 1).astype(F32)
    source = jnp.concatenate([lane8, other, key, key], axis=0).astype(BF16)
    moved = dot(source, place)
    order, other_sorted, key_sorted = moved[0:8], moved[8:16], moved[16:24]
    previous = pltpu.roll(key_sorted, 1, 1)
    keep = ((key_sorted == previous) & (lane8 > 0)).astype(F32)
    ones = jnp.ones((16, width), BF16)
    under = dot(ones, (key_i < lanes).astype(F32).astype(BF16))[0:8]
    upto = pltpu.roll(under, width - 1, 1)
    last = jnp.where(upto > under, upto - 1.0, float(empty))
    return order, other_sorted, keep, last


def kernel(
    far_rows_h,
    far_cols_h,
    link_rows_h,
    link_cols_h,
    local_rows_h,
    local_cols_h,
    cost_h,
    first_cost_h,
    first_h,
    local_h,
    far_h,
    link_h,
    inflow_h,
    rec_h,
    dual_h,
    first_out,
    rec_out,
    dual_out,
    far_rows_s,
    far_cols_s,
    link_rows_s,
    link_cols_s,
    local_rows_v,
    local_cols_v,
    far_rows_v,
    cost_v,
    first_own,
    first_own_cost,
    first_recv,
    first_full,
    first_cost,
    tiles,
    far,
    far_t,
    link,
    inflow,
    rec,
    rec_base,
    rec_old,
    dual,
    dual_base,
    half,
    bars,
    run,
    run_far,
    run_want,
    product,
    link_lhs,
    link_img,
    table_v,
    table_far_v,
    table_want_v,
    table,
    table_far,
    table_want,
    idx_send,
    idx_recv,
    term_send,
    term_recv,
    col_send,
    col_recv,
    z_recv,
    b_recv,
    load_sem,
    out_sem,
    idx_sem,
    sems,
):
    me_s = lax.axis_index("scen")
    me_b = lax.axis_index("blk")
    mx, my, mc = me_b // 8, (me_b // 2) % 4, me_b % 2

    def peer(step):
        jx, jy, jc = step
        return (((mx + jx) % 4) * 4 + (my + jy) % 4) * 2 + (mc + jc) % 2

    def source(step):
        return peer(tuple(-d for d in step))

    def group_peer(k):
        return (me_s + k // 2) % NS, me_b - mc + (mc + k) % 2

    barrier = pltpu.get_barrier_semaphore()

    def greet(step):
        pl.semaphore_signal(barrier, inc=1, device_id=(me_s, peer(step)), device_id_type=MESH)

    for step in ORDER[:-1]:
        greet(step)

    def greet_z(k, c):
        z, b = group_peer(k)
        pl.semaphore_signal(barrier, inc=1, device_id=(z, b), device_id_type=MESH)
        return c

    lax.fori_loop(2, 2 * NS, greet_z, 0)

    def load(src, dst, i):
        copy = pltpu.make_async_copy(src, dst, load_sem.at[i])
        copy.start()
        return copy

    load_rows = load(local_rows_h, local_rows_v, 0)
    load_cols = load(local_cols_h, local_cols_v, 1)
    load_far_rows_v = load(far_rows_h, far_rows_v, 2)
    load_far_rows = load(far_rows_h, far_rows_s, 3)
    load_far_cols = load(far_cols_h, far_cols_s, 4)
    load_dual = load(dual_h, dual, 5)
    load_far = load(far_h, far, 6)
    load_link_rows = load(link_rows_h, link_rows_s, 7)
    load_link_cols = load(link_cols_h, link_cols_s, 8)
    load_link = load(link_h, link, 9)
    load_first = load(first_h, first_own, 10)
    load_first_cost = load(first_cost_h, first_own_cost, 11)
    load_tiles = load(local_h, tiles, 12)
    load_cost = load(cost_h, cost_v, 13)
    load_rec = load(rec_h, rec, 14)
    load_inflow = load(inflow_h, inflow, 15)

    load_rows.wait()
    load_cols.wait()
    load_far_rows_v.wait()
    pad = jnp.full((8, W - NL), 64.0, F32)
    row_key = jnp.concatenate(
        [jnp.broadcast_to(local_rows_v[...].astype(F32), (8, NL)), pad], axis=1
    )
    col_key = jnp.concatenate(
        [jnp.broadcast_to(local_cols_v[...].astype(F32), (8, NL)), pad], axis=1
    )
    pad_far = jnp.full((8, WF - NF), 64.0, F32)
    far_key = jnp.concatenate(
        [jnp.broadcast_to(far_rows_v[...].astype(F32), (8, NF)), pad_far], axis=1
    )
    col_tables = sorted_tables(col_key, row_key, NL, W, NL)
    row_tables = sorted_tables(row_key, col_key, NL, W, NL)
    for i, value in enumerate(col_tables + row_tables):
        table_v[i : i + 1, :] = whole(value, LIMITS[i])
    far_tables = sorted_tables(far_key, far_key, NF, WF, NF)
    for i, value in enumerate(far_tables):
        table_far_v[i : i + 1, :] = whole(value, FAR_LIMITS[i])
    to_smem = [load(table_v, table, 0), load(table_far_v, table_far, 1)]
    zero = jnp.zeros((S, TILE), F32)
    run[NL] = zero
    run_far[NF] = zero
    run_want[NF] = zero

    load_dual.wait()

    def first_half(rb, c):
        half[rb] = dual[:, pl.ds(pl.multiple_of(rb * TILE, TILE), TILE)].astype(BF16)
        return c

    lax.fori_loop(0, RB, first_half, 0, unroll=8)
    load_far_rows.wait()
    load_far.wait()

    def send_all(it, src, dst, which):
        def one(i):
            p = peer(ORDER[i])
            group = [i in g for g in GROUPS].index(True)
            pltpu.make_async_remote_copy(
                src_ref=src.at[it, p],
                dst_ref=dst.at[it, me_b],
                send_sem=sems.at[it, which, 3],
                recv_sem=sems.at[it, which, group],
                device_id=(me_s, p),
                device_id_type=MESH,
            ).start()

        return one

    def bytes_of(buffer, count, sem):
        view = buffer.at[pl.ds(0, count)]
        pltpu.make_async_copy(view, view, sem).wait()

    def new_duals(r, last):
        return dual_base[r] - DUAL * (run_far[last] + link_img[pl.ds(r, 1), :])

    def new_recourse(b, last):
        new = jnp.maximum(rec_base[b] + PRIMAL * run_want[last], 0.0)
        return new, (2.0 * new - rec_old[b]).astype(BF16)

    for it in range(ITERS):
        send_term = send_all(it, term_send, term_recv, 0)
        for g in range(0, NB, 8):
            for step in ORDER[g : g + 8]:
                p = peer(step)
                r = far_rows_s[0, p]
                if it == 0:
                    value = half[r]
                else:
                    value = new_duals(r, table_far[3, r]).astype(BF16)
                term_send[it, p] = dot(value, far[p]).astype(BF16)
            if it == 0 and g == 0:
                pl.semaphore_wait(barrier, NB - 1 + 2 * NS - 2)
            for i in range(g, min(g + 8, NB - 1)):
                send_term(i)
        term_recv[it, me_b] = term_send[it, me_b]

        def to_half(rb, c):
            new = new_duals(rb, table_far[3, rb])
            dual[:, pl.ds(pl.multiple_of(rb * TILE, TILE), TILE)] = new
            half[rb] = new.astype(BF16)
            return c

        if it > 0:
            lax.fori_loop(0, RB, to_half, 0, unroll=8)

        if it == 0:
            load_far_cols.wait()
            for p in range(NB):
                idx_send[p] = jnp.full((1, TILE), far_cols_s[0, p], jnp.int32)
            for step in ORDER[:-1]:
                p = peer(step)
                pltpu.make_async_remote_copy(
                    src_ref=idx_send.at[p],
                    dst_ref=idx_recv.at[me_b],
                    send_sem=idx_sem.at[0],
                    recv_sem=idx_sem.at[1],
                    device_id=(me_s, p),
                    device_id_type=MESH,
                ).start()
            load_first.wait()
            load_first_cost.wait()
            first_recv[me_s, 0:XB] = first_own[...]
            first_recv[me_s, XB : 2 * XB] = first_own_cost[...]
            first_recv[me_s, 2 * XB :] = jnp.zeros((8 - 2 * XB, TILE), F32)

            def send_first(k, c):
                pltpu.make_async_remote_copy(
                    src_ref=first_recv.at[me_s],
                    dst_ref=first_recv.at[me_s],
                    send_sem=idx_sem.at[2],
                    recv_sem=idx_sem.at[3],
                    device_id=((me_s + k) % NS, me_b),
                    device_id_type=MESH,
                ).start()
                return c

            lax.fori_loop(1, NS, send_first, 0)
            load_link_rows.wait()
            load_link_cols.wait()
            load_link.wait()

        for n in range(NK):
            link_lhs[n : n + 1, :] = jnp.sum(
                half[link_rows_s[0, n]].astype(F32), axis=0, keepdims=True
            )
        sums = link_lhs[...]
        high = sums.astype(BF16)
        low = (sums - high.astype(F32)).astype(BF16)
        lhs = jnp.concatenate([high, low], axis=0)
        block = lax.broadcasted_iota(jnp.int32, (FB, TILE), 0)
        part = jnp.zeros((FB, TILE), F32)
        for n in range(NK):
            both = dot(lhs, link[n])
            row = both[n : n + 1] + both[NK + n : NK + n + 1]
            part = part + jnp.where(block == link_cols_s[0, n], row, 0.0)
        own = me_s * 2 + mc
        z_recv[it, own] = part.astype(BF16)

        def send_z(k, c):
            z, b = group_peer(k)
            pltpu.make_async_remote_copy(
                src_ref=z_recv.at[it, own],
                dst_ref=z_recv.at[it, own],
                send_sem=sems.at[it, 1, 0],
                recv_sem=sems.at[it, 1, 1],
                device_id=(z, b),
                device_id_type=MESH,
            ).start()
            return c

        lax.fori_loop(1, 2 * NS, send_z, 0)

        if it == 0:
            for copy in to_smem:
                copy.wait()
            load_tiles.wait()

        def gradient_step(n, total):
            keep = table[2, n].astype(F32)
            total = total * keep + dot(half[table[1, n]], tiles[table[0, n]])
            run[n] = total
            return total

        lax.fori_loop(0, NL, gradient_step, zero, unroll=UNROLL)

        if it == 0:
            load_rec.wait()
            load_cost.wait()

        def base_recourse(cb, c):
            at = pl.ds(pl.multiple_of(cb * TILE, TILE), TILE)
            old = rec[:, at]
            rec_old[cb] = old
            rec_base[cb] = old - PRIMAL * (cost_v[:, at] - run[table[3, cb]])
            return c

        lax.fori_loop(0, CB, base_recourse, 0, unroll=8)

        if it == 0:

            def turn(q, c):
                far_t[q] = far[q].T
                return c

            lax.fori_loop(0, NF, turn, 0, unroll=8)

            bytes_of(idx_recv, NB - 1, idx_sem.at[1])
            idx_recv[me_b] = idx_send[me_b]
            lane = lax.broadcasted_iota(jnp.int32, (1, WF), 1)
            wanted = jnp.full((1, WF), 64, jnp.int32)
            for q in range(NB):
                wanted = jnp.where(lane == q, idx_recv[q], wanted)
            want_key = jnp.broadcast_to(wanted.astype(F32), (8, WF))
            want_tables = sorted_tables(want_key, want_key, NF, WF, NF)
            for i, value in enumerate(want_tables):
                table_want_v[i : i + 1, :] = whole(value, FAR_LIMITS[i])
            table_want_v[1:2, :] = jnp.minimum(wanted, CB - 1)
            load(table_want_v, table_want, 0).wait()

        bytes_of(z_recv.at[it], 2 * NS - 1, sems.at[it, 1, 1])
        total = z_recv[it, 0].astype(F32)
        for k in range(1, 2 * NS):
            total = total + z_recv[it, k].astype(F32)
        place = me_b // 2
        b_recv[it, place] = total.astype(BF16)
        for step in STEPS[:-1]:
            pltpu.make_async_remote_copy(
                src_ref=b_recv.at[it, place],
                dst_ref=b_recv.at[it, place],
                send_sem=sems.at[it, 3, 0],
                recv_sem=sems.at[it, 3, 1],
                device_id=(me_s, peer(step + (0,))),
                device_id_type=MESH,
            ).start()

        for i, g in enumerate(GROUPS):
            bytes_of(term_recv.at[it], len(g), sems.at[it, 0, i])

        def want_step(k, total):
            keep = table_want[2, k].astype(F32)
            total = total * keep + term_recv[it, table_want[0, k]].astype(F32)
            run_want[k] = total
            return total

        lax.fori_loop(0, NF, want_step, zero, unroll=16)

        send_col = send_all(it, col_send, col_recv, 2)
        for g in range(0, NB, 8):
            for step in ORDER[g : g + 8]:
                p = peer(step)
                w = table_want[1, p]
                col_send[it, p] = new_recourse(w, table_want[3, w])[1]
            for i in range(g, min(g + 8, NB - 1)):
                send_col(i)
        col_recv[it, me_b] = col_send[it, me_b]

        def update_recourse(cb, c):
            new, bar = new_recourse(cb, table_want[3, cb])
            bars[cb] = bar
            rec[:, pl.ds(pl.multiple_of(cb * TILE, TILE), TILE)] = new
            return c

        lax.fori_loop(0, CB, update_recourse, 0, unroll=8)
        if it == ITERS - 1:
            store_rec = pltpu.make_async_copy(rec, rec_out, out_sem.at[0])
            store_rec.start()

        def image_step(n, total):
            keep = table[6, n].astype(F32)
            total = total * keep + dot_t(bars[table[5, n]], tiles[table[4, n]])
            run[n] = total
            return total

        lax.fori_loop(0, NL, image_step, zero, unroll=UNROLL)
        if it == 0:
            load_inflow.wait()

        def base_duals(rb, c):
            at = pl.ds(pl.multiple_of(rb * TILE, TILE), TILE)
            dual_base[rb] = dual[:, at] + DUAL * (
                inflow[:, at].astype(F32) - run[table[7, rb]]
            )
            return c

        lax.fori_loop(0, RB, base_duals, 0, unroll=8)

        if it == 0:
            bytes_of(first_recv, NS - 1, idx_sem.at[3])
            for s in range(NS):
                first_full[s * XB : (s + 1) * XB, :] = first_recv[s, 0:XB]
                first_cost[s * XB : (s + 1) * XB, :] = first_recv[s, XB : 2 * XB]
        bytes_of(b_recv.at[it], NB // 2 - 1, sems.at[it, 3, 1])
        total = b_recv[it, 0].astype(F32)
        for k in range(1, NB // 2):
            total = total + b_recv[it, k].astype(F32)
        old_first = first_full[...]
        new_first = jnp.maximum(
            old_first - FIRST * (first_cost[...] - total / (S * NS)), 0.0
        )
        first_full[...] = new_first
        if it == ITERS - 1:
            for i in range(XB):
                first_own[i : i + 1, :] = first_full[pl.ds(me_s * XB + i, 1), :]
            store_first = pltpu.make_async_copy(first_own, first_out, out_sem.at[1])
            store_first.start()

        link_img[0:FB, :] = 2.0 * new_first - old_first
        for n in range(NK):
            link_lhs[n : n + 1, :] = link_img[pl.ds(link_cols_s[0, n], 1), :]
        lhs = link_lhs[...].astype(BF16)
        block = lax.broadcasted_iota(jnp.int32, (RB, TILE), 0)
        image = jnp.zeros((RB, TILE), F32)
        for n in range(NK):
            row = dot_t(lhs, link[n])[n : n + 1]
            image = image + jnp.where(block == link_rows_s[0, n], row, 0.0)
        link_img[...] = image

        product[me_b] = dot(col_recv[it, me_b], far_t[me_b])
        for i in (2, 1, 0):
            g = GROUPS[i]
            bytes_of(col_recv.at[it], len(g), sems.at[it, 2, i])
            for k in g:
                q = source(ORDER[k])
                product[q] = dot(col_recv[it, q], far_t[q])

        def far_step(k, total):
            total = total * table_far[2, k].astype(F32) + product[table_far[0, k]]
            run_far[k] = total
            return total

        lax.fori_loop(0, NF, far_step, zero, unroll=32)

    parts = []
    for part in range(2):

        def update_duals(rb, c):
            at = pl.ds(pl.multiple_of(rb * TILE, TILE), TILE)
            dual[:, at] = new_duals(rb, table_far[3, rb])
            return c

        lax.fori_loop(part * RB // 2, (part + 1) * RB // 2, update_duals, 0, unroll=10)
        at = pl.ds(part * RB // 2 * TILE, RB // 2 * TILE)
        copy = pltpu.make_async_copy(dual.at[:, at], dual_out.at[:, at], out_sem.at[2 + part])
        copy.start()
        parts.append(copy)
    bytes_of(idx_recv, NB - 1, idx_sem.at[0])
    bytes_of(first_recv, NS - 1, idx_sem.at[2])
    for it in range(ITERS):
        bytes_of(term_recv.at[it], NB - 1, sems.at[it, 0, 3])
        bytes_of(z_recv.at[it], 2 * NS - 1, sems.at[it, 1, 0])
        bytes_of(col_recv.at[it], NB - 1, sems.at[it, 2, 3])
        bytes_of(b_recv.at[it], NB // 2 - 1, sems.at[it, 3, 0])
    store_rec.wait()
    store_first.wait()
    for copy in parts:
        copy.wait()


def hand_out(first, rec, dual, first_out, rec_out, dual_out):
    first_out[...] = first[...]
    rec_out[...] = rec[...]
    dual_out[...] = dual[...]


def body(
    local_tiles,
    local_rows,
    local_cols,
    far_tiles,
    far_rows,
    far_cols,
    link_tiles,
    link_rows,
    link_cols,
    inflows,
    recourse_cost,
    first_cost,
    first_section,
    recourse,
    duals,
):
    hbm = pl.BlockSpec(memory_space=pltpu.HBM)
    dma = pltpu.SemaphoreType.DMA
    vmem, smem = pltpu.VMEM, pltpu.SMEM
    int32 = jnp.int32
    shapes = (
        jax.ShapeDtypeStruct((XB, TILE), F32),
        jax.ShapeDtypeStruct((S, CB * TILE), F32),
        jax.ShapeDtypeStruct((S, RB * TILE), F32),
    )
    results = pl.pallas_call(
        kernel,
        out_shape=shapes,
        in_specs=[hbm] * 15,
        out_specs=(hbm, hbm, hbm),
        scratch_shapes=[
            smem((1, NF), int32),
            smem((1, NF), int32),
            smem((1, NK), int32),
            smem((1, NK), int32),
            vmem((1, NL), int32),
            vmem((1, NL), int32),
            vmem((1, NF), int32),
            vmem((1, CB * TILE), F32),
            vmem((XB, TILE), F32),
            vmem((XB, TILE), F32),
            vmem((NS, 8, TILE), F32),
            vmem((FB, TILE), F32),
            vmem((FB, TILE), F32),
            vmem((NL, TILE, TILE), BF16),
            vmem((NF, TILE, TILE), BF16),
            vmem((NF, TILE, TILE), BF16),
            vmem((NK, TILE, TILE), BF16),
            vmem((S, RB * TILE), BF16),
            vmem((S, CB * TILE), F32),
            vmem((CB, S, TILE), F32),
            vmem((CB, S, TILE), F32),
            vmem((S, RB * TILE), F32),
            vmem((RB, S, TILE), F32),
            vmem((RB, S, TILE), BF16),
            vmem((CB, S, TILE), BF16),
            vmem((NL + 1, S, TILE), F32),
            vmem((NF + 1, S, TILE), F32),
            vmem((NF + 1, S, TILE), F32),
            vmem((NF, S, TILE), F32),
            vmem((NK, TILE), F32),
            vmem((RB, TILE), F32),
            vmem((8, W), int32),
            vmem((4, WF), int32),
            vmem((4, WF), int32),
            smem((8, W), int32),
            smem((4, WF), int32),
            smem((4, WF), int32),
            vmem((NB, 1, TILE), int32),
            vmem((NB, 1, TILE), int32),
            vmem((ITERS, NB, S, TILE), BF16),
            vmem((ITERS, NB, S, TILE), BF16),
            vmem((ITERS, NB, S, TILE), BF16),
            vmem((ITERS, NB, S, TILE), BF16),
            vmem((ITERS, 2 * NS, FB, TILE), BF16),
            vmem((ITERS, NB // 2, FB, TILE), BF16),
            dma((16,)),
            dma((4,)),
            dma((4,)),
            dma((ITERS, 4, 4)),
        ],
        compiler_params=pltpu.CompilerParams(
            collective_id=0, has_side_effects=True, vmem_limit_bytes=62 << 20
        ),
        name="dispatch",
    )(
        far_rows.reshape(1, NF),
        far_cols.reshape(1, NF),
        link_rows.reshape(1, NK),
        link_cols.reshape(1, NK),
        local_rows.reshape(1, NL),
        local_cols.reshape(1, NL),
        recourse_cost.reshape(1, CB * TILE),
        first_cost.reshape(XB, TILE),
        first_section.reshape(XB, TILE),
        local_tiles,
        far_tiles.reshape(NF, TILE, TILE),
        link_tiles,
        inflows,
        recourse,
        duals,
    )
    first_out, rec_out, dual_out = pl.pallas_call(
        hand_out,
        out_shape=shapes,
        in_specs=[pl.BlockSpec(memory_space=vmem)] * 3,
        out_specs=[pl.BlockSpec(memory_space=vmem)] * 3,
        compiler_params=pltpu.CompilerParams(vmem_limit_bytes=62 << 20),
        name="hand_out",
    )(*results)
    return first_out.reshape(XB * TILE), rec_out, dual_out


def solution(mesh):
    in_specs = (
        P("blk", None, None),
        P("blk"),
        P("blk"),
        P("blk", None, None, None),
        P("blk", None),
        P("blk", None),
        P(("scen", "blk"), None, None),
        P(("scen", "blk")),
        P(("scen", "blk")),
        P("scen", "blk"),
        P("blk"),
        P("scen"),
        P("scen"),
        P("scen", "blk"),
        P("scen", "blk"),
    )
    out_specs = (P("scen"), P("scen", "blk"), P("scen", "blk"))
    return jax.shard_map(body, mesh=mesh, in_specs=in_specs, out_specs=out_specs, check_vma=False)
```

```python
import functools

import jax
import jax.numpy as jnp
from jax import lax
from jax.experimental import pallas as pl
from jax.experimental.pallas import tpu as pltpu
from jax.sharding import PartitionSpec as P

TILE = 128
ITERS = 2
S = 32
RB = 40
CB = 32
NL = 224
NF = 32
NK = 16
XB = 2
NS = 8
NB = 32
FB = XB * NS
W = 256
WF = 128
STEPS = sorted(
    ((a, b) for a in range(4) for b in range(4)),
    key=lambda d: -(min(d[0], 4 - d[0]) + min(d[1], 4 - d[1])),
)
ORDER = [(a, b, c) for c in (1, 0) for a, b in STEPS]
GROUPS = tuple(
    tuple(i for i in range(NB - 1) if i % 16 in part)
    for part in (range(0, 5), range(5, 11), range(11, 16))
)
TAKE = [NB - 1] + [i for part in GROUPS[::-1] for i in part]
UNROLL = 56

PRIMAL = 0.4
FIRST = 2.0
DUAL = 0.4
COL_LIMITS = (NL - 1, RB - 1, 1, NL)
ROW_LIMITS = (NL - 1, CB - 1, 1, NL)
MESH = pl.DeviceIdType.MESH
F32 = jnp.float32
BF16 = jnp.bfloat16


def dot(a, b):
    return jnp.dot(a, b, preferred_element_type=F32)


def dot_t(a, b):
    return lax.dot_general(a, b, (((1,), (1,)), ((), ())), preferred_element_type=F32)


def whole(value, top):
    return jnp.clip(value[0:1].astype(jnp.int32), 0, top)


def chain_tables(column, key):
    rows = lax.broadcasted_iota(jnp.int32, (NF, WF), 0)
    lanes = lax.broadcasted_iota(jnp.int32, (NF, WF), 1)
    result = []
    for hit in ((column == key) & (rows < lanes), column == lanes):
        top = jnp.max(jnp.where(hit, rows + 1, 0), axis=0, keepdims=True)
        result.append(jnp.where(top == 0, NF, top - 1))
    return result


def sorted_tables(key, other, count, width, empty):
    rows = lax.broadcasted_iota(jnp.int32, (width, width), 0).astype(F32)
    lanes = lax.broadcasted_iota(jnp.int32, (width, width), 1).astype(F32)
    key_j = jnp.broadcast_to(key[0:1], (width, width))
    key_i = key_j.T
    before = (key_j * W + lanes) < (key_i * W + rows)
    rank = dot(before.astype(F32).astype(BF16), jnp.ones((width, width), BF16))
    place = (rank == lanes).astype(F32).astype(BF16)
    lane8 = lax.broadcasted_iota(jnp.int32, (8, width), 1).astype(F32)
    source = jnp.concatenate([lane8, other, key, key], axis=0).astype(BF16)
    moved = dot(source, place)
    order, other_sorted, key_sorted = moved[0:8], moved[8:16], moved[16:24]
    previous = pltpu.roll(key_sorted, 1, 1)
    keep = ((key_sorted == previous) & (lane8 > 0)).astype(F32)
    ones = jnp.ones((16, width), BF16)
    under = dot(ones, (key_i < lanes).astype(F32).astype(BF16))[0:8]
    upto = pltpu.roll(under, width - 1, 1)
    last = jnp.where(upto > under, upto - 1.0, float(empty))
    return order, other_sorted, keep, last


def kernel(
    far_rows_h,
    far_cols_h,
    link_rows_h,
    link_cols_h,
    local_rows_h,
    local_cols_h,
    cost_h,
    first_cost_h,
    first_h,
    local_h,
    far_h,
    link_h,
    inflow_h,
    rec_h,
    dual_h,
    first_out,
    rec,
    dual,
    far_rows_s,
    far_cols_s,
    link_rows_s,
    link_cols_s,
    local_rows_v,
    local_cols_v,
    cost_v,
    first_own,
    first_own_cost,
    first_recv,
    first_full,
    first_cost,
    tiles,
    far,
    far_t,
    link,
    inflow,
    rec_base,
    rec_old,
    dual_base,
    half,
    bars,
    run,
    run_far,
    run_want,
    link_lhs,
    link_img,
    table_col_v,
    table_row_v,
    table_far_v,
    table_want_v,
    chain_v,
    table_col,
    table_row,
    table_far,
    table_want,
    idx_send,
    idx_recv,
    term_send,
    term_recv,
    col_send,
    col_recv,
    z_recv,
    b_recv,
    load_sem,
    idx_sem,
    sems,
):
    me_s = lax.axis_index("scen")
    me_b = lax.axis_index("blk")
    mx, my, mc = me_b // 8, (me_b // 2) % 4, me_b % 2

    def peer(step):
        jx, jy, jc = step
        return (((mx + jx) % 4) * 4 + (my + jy) % 4) * 2 + (mc + jc) % 2

    def source(step):
        return peer(tuple(-d for d in step))

    def taken(step):
        back = tuple(-d % n for d, n in zip(step, (4, 4, 2)))
        return TAKE.index(ORDER.index(back))

    def group_peer(k):
        return (me_s + k // 2) % NS, me_b - mc + (mc + k) % 2

    barrier = pltpu.get_barrier_semaphore()

    def greet(step):
        pl.semaphore_signal(barrier, inc=1, device_id=(me_s, peer(step)), device_id_type=MESH)

    for step in ORDER[:-1]:
        greet(step)

    def greet_z(k, c):
        z, b = group_peer(k)
        pl.semaphore_signal(barrier, inc=1, device_id=(z, b), device_id_type=MESH)
        return c

    lax.fori_loop(2, 2 * NS, greet_z, 0)

    def load(src, dst, i):
        copy = pltpu.make_async_copy(src, dst, load_sem.at[i])
        copy.start()
        return copy

    load_dual = load(dual_h, dual, 5)
    load_far_rows = load(far_rows_h, far_rows_s, 3)
    load_far = load(far_h, far, 6)
    load_rows = load(local_rows_h, local_rows_v, 0)
    load_cols = load(local_cols_h, local_cols_v, 1)
    load_far_cols = load(far_cols_h, far_cols_s, 4)
    load_link_rows = load(link_rows_h, link_rows_s, 7)
    load_link_cols = load(link_cols_h, link_cols_s, 8)
    load_first = load(first_h, first_own, 10)
    load_first_cost = load(first_cost_h, first_own_cost, 11)

    zero = jnp.zeros((S, TILE), F32)
    run[NL] = zero
    run_far[NF] = zero
    run_want[NF] = zero

    load_dual.wait()

    def first_half(rb, c):
        half[rb] = dual[:, pl.ds(pl.multiple_of(rb * TILE, TILE), TILE)].astype(BF16)
        return c

    lax.fori_loop(0, RB, first_half, 0, unroll=8)
    load_far_rows.wait()
    load_far.wait()
    load_link = load(link_h, link, 9)
    load_tiles = load(local_h, tiles, 12)
    load_cost = load(cost_h, cost_v, 13)
    load_rec = load(rec_h, rec, 14)
    load_inflow = load(inflow_h, inflow, 15)

    def send_all(it, src, dst, which):
        def one(i):
            p = peer(ORDER[i])
            group = [i in g for g in GROUPS].index(True)
            pltpu.make_async_remote_copy(
                src_ref=src.at[it, p],
                dst_ref=dst.at[it, me_b],
                send_sem=sems.at[it, which, 3],
                recv_sem=sems.at[it, which, group],
                device_id=(me_s, p),
                device_id_type=MESH,
            ).start()

        return one

    def bytes_of(buffer, count, sem):
        view = buffer.at[pl.ds(0, count)]
        pltpu.make_async_copy(view, view, sem).wait()

    def new_duals(r, last):
        return dual_base[r] - DUAL * (run_far[last] + link_img[pl.ds(r, 1), :])

    def new_recourse(b, last):
        new = jnp.maximum(rec_base[b] + PRIMAL * run_want[last], 0.0)
        return new, (2.0 * new - rec_old[b]).astype(BF16)

    for it in range(ITERS):
        send_term = send_all(it, term_send, term_recv, 0)
        width = NB if it == 0 else 8
        for g in range(0, NB, width):
            for step in ORDER[g : g + width]:
                p = peer(step)
                r = far_rows_s[0, p]
                if it == 0:
                    value = half[r]
                else:
                    value = new_duals(r, table_far[1, r]).astype(BF16)
                term_send[it, p] = dot(value, far[p]).astype(BF16)
            if it == 0:
                pl.semaphore_wait(barrier, NB - 1 + 2 * NS - 2)
            for i in range(g, min(g + width, NB - 1)):
                send_term(i)
        term_recv[it, me_b] = term_send[it, me_b]

        def to_half(rb, c):
            new = new_duals(rb, table_far[1, rb])
            dual[:, pl.ds(pl.multiple_of(rb * TILE, TILE), TILE)] = new
            half[rb] = new.astype(BF16)
            return c

        if it > 0:
            lax.fori_loop(0, RB, to_half, 0, unroll=8)

        if it == 0:
            load_far_cols.wait()
            for p in range(NB):
                idx_send[p] = jnp.full((1, TILE), far_cols_s[0, p], jnp.int32)
            for step in ORDER[:-1]:
                p = peer(step)
                pltpu.make_async_remote_copy(
                    src_ref=idx_send.at[p],
                    dst_ref=idx_recv.at[me_b],
                    send_sem=idx_sem.at[0],
                    recv_sem=idx_sem.at[1],
                    device_id=(me_s, p),
                    device_id_type=MESH,
                ).start()
            load_first.wait()
            load_first_cost.wait()
            first_recv[me_s, 0:XB] = first_own[...]
            first_recv[me_s, XB : 2 * XB] = first_own_cost[...]
            first_recv[me_s, 2 * XB :] = jnp.zeros((8 - 2 * XB, TILE), F32)

            def send_first(k, c):
                pltpu.make_async_remote_copy(
                    src_ref=first_recv.at[me_s],
                    dst_ref=first_recv.at[me_s],
                    send_sem=idx_sem.at[2],
                    recv_sem=idx_sem.at[3],
                    device_id=((me_s + k) % NS, me_b),
                    device_id_type=MESH,
                ).start()
                return c

            lax.fori_loop(1, NS, send_first, 0)
            load_link_rows.wait()
            load_link_cols.wait()
            load_link.wait()

        for n in range(NK):
            link_lhs[n : n + 1, :] = jnp.sum(
                half[link_rows_s[0, n]].astype(F32), axis=0, keepdims=True
            )
        sums = link_lhs[...]
        high = sums.astype(BF16)
        low = (sums - high.astype(F32)).astype(BF16)
        lhs = jnp.concatenate([high, low], axis=0)
        block = lax.broadcasted_iota(jnp.int32, (FB, TILE), 0)
        part = jnp.zeros((FB, TILE), F32)
        for n in range(NK):
            both = dot(lhs, link[n])
            row = both[n : n + 1] + both[NK + n : NK + n + 1]
            part = part + jnp.where(block == link_cols_s[0, n], row, 0.0)
        own = me_s * 2 + mc
        z_recv[it, own] = part.astype(BF16)

        def send_z(k, c):
            z, b = group_peer(k)
            pltpu.make_async_remote_copy(
                src_ref=z_recv.at[it, own],
                dst_ref=z_recv.at[it, own],
                send_sem=sems.at[it, 1, 0],
                recv_sem=sems.at[it, 1, 1],
                device_id=(z, b),
                device_id_type=MESH,
            ).start()
            return c

        lax.fori_loop(1, 2 * NS, send_z, 0)

        if it == 0:
            load_rows.wait()
            load_cols.wait()
            pad = jnp.full((8, W - NL), 64.0, F32)
            row_key = jnp.concatenate(
                [jnp.broadcast_to(local_rows_v[...].astype(F32), (8, NL)), pad], axis=1
            )
            col_key = jnp.concatenate(
                [jnp.broadcast_to(local_cols_v[...].astype(F32), (8, NL)), pad], axis=1
            )
            col_tables = sorted_tables(col_key, row_key, NL, W, NL)
            for i, value in enumerate(col_tables):
                table_col_v[i : i + 1, :] = whole(value, COL_LIMITS[i])
            col_to_smem = load(table_col_v, table_col, 0)
            col_to_smem.wait()
            load_tiles.wait()

        def gradient_step(n, total):
            keep = table_col[2, n].astype(F32)
            total = total * keep + dot(half[table_col[1, n]], tiles[table_col[0, n]])
            run[n] = total
            return total

        lax.fori_loop(0, NL, gradient_step, zero, unroll=UNROLL)

        if it == 0:
            load_rec.wait()
            load_cost.wait()

        def base_recourse(cb, c):
            at = pl.ds(pl.multiple_of(cb * TILE, TILE), TILE)
            old = rec[:, at]
            rec_old[cb] = old
            rec_base[cb] = old - PRIMAL * (cost_v[:, at] - run[table_col[3, cb]])
            return c

        lax.fori_loop(0, CB, base_recourse, 0, unroll=8)

        if it == 0:

            def turn(q, c):
                far_t[q] = far[q].T
                return c

            lax.fori_loop(0, NF, turn, 0, unroll=8)

            row_tables = sorted_tables(row_key, col_key, NL, W, NL)
            for i, value in enumerate(row_tables):
                table_row_v[i : i + 1, :] = whole(value, ROW_LIMITS[i])
            row_to_smem = load(table_row_v, table_row, 1)

            lane = lax.broadcasted_iota(jnp.int32, (1, WF), 1)
            key = jnp.full((1, WF), 64, jnp.int32)
            for k, i in enumerate(TAKE):
                row = jnp.full((1, WF), far_rows_s[0, source(ORDER[i])], jnp.int32)
                chain_v[k : k + 1, :] = row
                key = jnp.where(lane == k, row, key)
            for i, value in enumerate(chain_tables(chain_v[...], key)):
                table_far_v[i : i + 1, :] = value
            far_to_smem = load(table_far_v, table_far, 2)

            bytes_of(idx_recv, NB - 1, idx_sem.at[1])
            idx_recv[me_b] = idx_send[me_b]
            key = jnp.full((1, WF), 64, jnp.int32)
            for k, i in enumerate(TAKE):
                row = idx_recv[source(ORDER[i])]
                chain_v[k : k + 1, :] = row
                key = jnp.where(lane == k, row, key)
            for i, value in enumerate(chain_tables(chain_v[...], key)):
                table_want_v[i : i + 1, :] = value
            table_want_v[2:3, :] = jnp.minimum(key, CB - 1)
            load(table_want_v, table_want, 0).wait()
            row_to_smem.wait()
            far_to_smem.wait()

        bytes_of(z_recv.at[it], 2 * NS - 1, sems.at[it, 1, 1])
        total = z_recv[it, 0].astype(F32)
        for k in range(1, 2 * NS):
            total = total + z_recv[it, k].astype(F32)
        place = me_b // 2
        b_recv[it, place] = total.astype(BF16)
        for step in STEPS[:-1]:
            pltpu.make_async_remote_copy(
                src_ref=b_recv.at[it, place],
                dst_ref=b_recv.at[it, place],
                send_sem=sems.at[it, 3, 0],
                recv_sem=sems.at[it, 3, 1],
                device_id=(me_s, peer(step + (0,))),
                device_id_type=MESH,
            ).start()

        for k, i in enumerate(TAKE):
            for j, g in enumerate(GROUPS):
                if i == g[0]:
                    bytes_of(term_recv.at[it], len(g), sems.at[it, 0, j])
            term = term_recv[it, source(ORDER[i])].astype(F32)
            run_want[k] = run_want[table_want[0, k]] + term

        send_col = send_all(it, col_send, col_recv, 2)
        for g in range(0, NB, 8):
            for step in ORDER[g : g + 8]:
                p = peer(step)
                w = table_want[2, taken(step)]
                col_send[it, p] = new_recourse(w, table_want[1, w])[1]
            for i in range(g, min(g + 8, NB - 1)):
                send_col(i)
        col_recv[it, me_b] = col_send[it, me_b]

        def update_recourse(cb, c):
            new, bar = new_recourse(cb, table_want[1, cb])
            bars[cb] = bar
            rec[:, pl.ds(pl.multiple_of(cb * TILE, TILE), TILE)] = new
            return c

        lax.fori_loop(0, CB, update_recourse, 0, unroll=8)

        def image_step(n, total):
            keep = table_row[2, n].astype(F32)
            total = total * keep + dot_t(bars[table_row[1, n]], tiles[table_row[0, n]])
            run[n] = total
            return total

        lax.fori_loop(0, NL, image_step, zero, unroll=UNROLL)
        if it == 0:
            load_inflow.wait()

        def base_duals(rb, c):
            at = pl.ds(pl.multiple_of(rb * TILE, TILE), TILE)
            dual_base[rb] = dual[:, at] + DUAL * (
                inflow[:, at].astype(F32) - run[table_row[3, rb]]
            )
            return c

        lax.fori_loop(0, RB, base_duals, 0, unroll=8)

        if it == 0:
            bytes_of(first_recv, NS - 1, idx_sem.at[3])
            for s in range(NS):
                first_full[s * XB : (s + 1) * XB, :] = first_recv[s, 0:XB]
                first_cost[s * XB : (s + 1) * XB, :] = first_recv[s, XB : 2 * XB]
        bytes_of(b_recv.at[it], NB // 2 - 1, sems.at[it, 3, 1])
        total = b_recv[it, 0].astype(F32)
        for k in range(1, NB // 2):
            total = total + b_recv[it, k].astype(F32)
        old_first = first_full[...]
        new_first = jnp.maximum(
            old_first - FIRST * (first_cost[...] - total / (S * NS)), 0.0
        )
        first_full[...] = new_first
        if it == ITERS - 1:
            for i in range(XB):
                first_out[i : i + 1, :] = first_full[pl.ds(me_s * XB + i, 1), :]

        link_img[0:FB, :] = 2.0 * new_first - old_first
        for n in range(NK):
            link_lhs[n : n + 1, :] = link_img[pl.ds(link_cols_s[0, n], 1), :]
        lhs = link_lhs[...].astype(BF16)
        block = lax.broadcasted_iota(jnp.int32, (RB, TILE), 0)
        image = jnp.zeros((RB, TILE), F32)
        for n in range(NK):
            row = dot_t(lhs, link[n])[n : n + 1]
            image = image + jnp.where(block == link_rows_s[0, n], row, 0.0)
        link_img[...] = image

        for k, i in enumerate(TAKE):
            for j, g in enumerate(GROUPS):
                if i == g[0]:
                    bytes_of(col_recv.at[it], len(g), sems.at[it, 2, j])
            q = source(ORDER[i])
            run_far[k] = run_far[table_far[0, k]] + dot(col_recv[it, q], far_t[q])

    def update_duals(rb, c):
        at = pl.ds(pl.multiple_of(rb * TILE, TILE), TILE)
        dual[:, at] = new_duals(rb, table_far[1, rb])
        return c

    lax.fori_loop(0, RB, update_duals, 0, unroll=10)
    bytes_of(idx_recv, NB - 1, idx_sem.at[0])
    bytes_of(first_recv, NS - 1, idx_sem.at[2])
    for it in range(ITERS):
        bytes_of(term_recv.at[it], NB - 1, sems.at[it, 0, 3])
        bytes_of(z_recv.at[it], 2 * NS - 1, sems.at[it, 1, 0])
        bytes_of(col_recv.at[it], NB - 1, sems.at[it, 2, 3])
        bytes_of(b_recv.at[it], NB // 2 - 1, sems.at[it, 3, 0])


def hand_out(first, rec, dual, first_out, rec_out, dual_out, sem):
    copies = [
        pltpu.make_async_copy(first, first_out, sem.at[0]),
        pltpu.make_async_copy(rec, rec_out, sem.at[1]),
        pltpu.make_async_copy(dual, dual_out, sem.at[2]),
    ]
    for copy in copies:
        copy.start()
    for copy in copies:
        copy.wait()


def body(
    local_tiles,
    local_rows,
    local_cols,
    far_tiles,
    far_rows,
    far_cols,
    link_tiles,
    link_rows,
    link_cols,
    inflows,
    recourse_cost,
    first_cost,
    first_section,
    recourse,
    duals,
):
    hbm = pl.BlockSpec(memory_space=pltpu.HBM)
    dma = pltpu.SemaphoreType.DMA
    vmem, smem = pltpu.VMEM, pltpu.SMEM
    int32 = jnp.int32
    shapes = (
        jax.ShapeDtypeStruct((XB, TILE), F32),
        jax.ShapeDtypeStruct((S, CB * TILE), F32),
        jax.ShapeDtypeStruct((S, RB * TILE), F32),
    )
    held = [vmem(shape.shape, F32) for shape in shapes]
    results = pl.pallas_call(
        kernel,
        out_shape=held,
        in_specs=[hbm] * 15,
        out_specs=[pl.BlockSpec(memory_space=vmem)] * 3,
        scratch_shapes=[
            smem((1, NF), int32),
            smem((1, NF), int32),
            smem((1, NK), int32),
            smem((1, NK), int32),
            vmem((1, NL), int32),
            vmem((1, NL), int32),
            vmem((1, CB * TILE), F32),
            vmem((XB, TILE), F32),
            vmem((XB, TILE), F32),
            vmem((NS, 8, TILE), F32),
            vmem((FB, TILE), F32),
            vmem((FB, TILE), F32),
            vmem((NL, TILE, TILE), BF16),
            vmem((NF, TILE, TILE), BF16),
            vmem((NF, TILE, TILE), BF16),
            vmem((NK, TILE, TILE), BF16),
            vmem((S, RB * TILE), BF16),
            vmem((CB, S, TILE), F32),
            vmem((CB, S, TILE), F32),
            vmem((RB, S, TILE), F32),
            vmem((RB, S, TILE), BF16),
            vmem((CB, S, TILE), BF16),
            vmem((NL + 1, S, TILE), F32),
            vmem((NF + 1, S, TILE), F32),
            vmem((NF + 1, S, TILE), F32),
            vmem((NK, TILE), F32),
            vmem((RB, TILE), F32),
            vmem((4, W), int32),
            vmem((4, W), int32),
            vmem((2, WF), int32),
            vmem((3, WF), int32),
            vmem((NF, WF), int32),
            smem((4, W), int32),
            smem((4, W), int32),
            smem((2, WF), int32),
            smem((3, WF), int32),
            vmem((NB, 1, TILE), int32),
            vmem((NB, 1, TILE), int32),
            vmem((ITERS, NB, S, TILE), BF16),
            vmem((ITERS, NB, S, TILE), BF16),
            vmem((ITERS, NB, S, TILE), BF16),
            vmem((ITERS, NB, S, TILE), BF16),
            vmem((ITERS, 2 * NS, FB, TILE), BF16),
            vmem((ITERS, NB // 2, FB, TILE), BF16),
            dma((16,)),
            dma((4,)),
            dma((ITERS, 4, 4)),
        ],
        compiler_params=pltpu.CompilerParams(
            collective_id=0, has_side_effects=True, vmem_limit_bytes=60 << 20
        ),
        name="dispatch",
    )(
        far_rows.reshape(1, NF),
        far_cols.reshape(1, NF),
        link_rows.reshape(1, NK),
        link_cols.reshape(1, NK),
        local_rows.reshape(1, NL),
        local_cols.reshape(1, NL),
        recourse_cost.reshape(1, CB * TILE),
        first_cost.reshape(XB, TILE),
        first_section.reshape(XB, TILE),
        local_tiles,
        far_tiles.reshape(NF, TILE, TILE),
        link_tiles,
        inflows,
        recourse,
        duals,
    )
    first_out, rec_out, dual_out = pl.pallas_call(
        hand_out,
        out_shape=shapes,
        in_specs=[pl.BlockSpec(memory_space=vmem)] * 3,
        out_specs=(hbm, hbm, hbm),
        scratch_shapes=[dma((3,))],
        compiler_params=pltpu.CompilerParams(vmem_limit_bytes=60 << 20),
        name="hand_out",
    )(*(pltpu.with_memory_space_constraint(result, vmem) for result in results))
    return first_out.reshape(XB * TILE), rec_out, dual_out


def solution(mesh):
    in_specs = (
        P("blk", None, None),
        P("blk"),
        P("blk"),
        P("blk", None, None, None),
        P("blk", None),
        P("blk", None),
        P(("scen", "blk"), None, None),
        P(("scen", "blk")),
        P(("scen", "blk")),
        P("scen", "blk"),
        P("blk"),
        P("scen"),
        P("scen"),
        P("scen", "blk"),
        P("scen", "blk"),
    )
    out_specs = (P("scen"), P("scen", "blk"), P("scen", "blk"))
    return jax.shard_map(body, mesh=mesh, in_specs=in_specs, out_specs=out_specs, check_vma=False)
```

```python
import functools

import jax
import jax.numpy as jnp
from jax import lax
from jax.experimental import pallas as pl
from jax.experimental.pallas import tpu as pltpu
from jax.sharding import PartitionSpec as P

TILE = 128
ITERS = 2
S = 32
RB = 40
CB = 32
NL = 224
NF = 32
NK = 16
XB = 2
NS = 8
NB = 32
FB = XB * NS
W = 256
WF = 128
STEPS = sorted(
    ((a, b) for a in range(4) for b in range(4)),
    key=lambda d: -(min(d[0], 4 - d[0]) + min(d[1], 4 - d[1])),
)
ORDER = [(a, b, c) for c in (1, 0) for a, b in STEPS]
GROUPS = tuple(
    tuple(i for i in range(NB - 1) if i % 16 in part)
    for part in (range(0, 5), range(5, 11), range(11, 16))
)
TAKE = [NB - 1] + [i for part in GROUPS[::-1] for i in part]
UNROLL = 56

PRIMAL = 0.4
FIRST = 2.0
DUAL = 0.4
COL_LIMITS = (NL - 1, RB - 1, 1, NL)
ROW_LIMITS = (NL - 1, CB - 1, 1, NL)
MESH = pl.DeviceIdType.MESH
F32 = jnp.float32
BF16 = jnp.bfloat16


def dot(a, b):
    return jnp.dot(a, b, preferred_element_type=F32)


def dot_t(a, b):
    return lax.dot_general(a, b, (((1,), (1,)), ((), ())), preferred_element_type=F32)


def whole(value, top):
    return jnp.clip(value[0:1].astype(jnp.int32), 0, top)


def chain_tables(column, key):
    rows = lax.broadcasted_iota(jnp.int32, (NF, WF), 0)
    lanes = lax.broadcasted_iota(jnp.int32, (NF, WF), 1)
    result = []
    for hit in ((column == key) & (rows < lanes), column == lanes):
        top = jnp.max(jnp.where(hit, rows + 1, 0), axis=0, keepdims=True)
        result.append(jnp.where(top == 0, NF, top - 1))
    return result


def sorted_tables(key, other, count, width, empty):
    rows = lax.broadcasted_iota(jnp.int32, (width, width), 0).astype(F32)
    lanes = lax.broadcasted_iota(jnp.int32, (width, width), 1).astype(F32)
    key_j = jnp.broadcast_to(key[0:1], (width, width))
    key_i = key_j.T
    before = (key_j * W + lanes) < (key_i * W + rows)
    rank = dot(before.astype(F32).astype(BF16), jnp.ones((width, width), BF16))
    place = (rank == lanes).astype(F32).astype(BF16)
    lane8 = lax.broadcasted_iota(jnp.int32, (8, width), 1).astype(F32)
    source = jnp.concatenate([lane8, other, key, key], axis=0).astype(BF16)
    moved = dot(source, place)
    order, other_sorted, key_sorted = moved[0:8], moved[8:16], moved[16:24]
    previous = pltpu.roll(key_sorted, 1, 1)
    keep = ((key_sorted == previous) & (lane8 > 0)).astype(F32)
    ones = jnp.ones((16, width), BF16)
    under = dot(ones, (key_i < lanes).astype(F32).astype(BF16))[0:8]
    upto = pltpu.roll(under, width - 1, 1)
    last = jnp.where(upto > under, upto - 1.0, float(empty))
    return order, other_sorted, keep, last


def kernel(
    far_rows_h,
    far_cols_h,
    link_rows_h,
    link_cols_h,
    local_rows_h,
    local_cols_h,
    cost_h,
    first_cost_h,
    first_h,
    local_h,
    far_h,
    link_h,
    inflow_h,
    rec_h,
    dual_h,
    first_out,
    rec,
    dual,
    far_rows_s,
    far_cols_s,
    link_rows_s,
    link_cols_s,
    local_rows_v,
    local_cols_v,
    cost_v,
    first_own,
    first_own_cost,
    first_recv,
    first_full,
    first_cost,
    tiles,
    tiles_t,
    far,
    far_t,
    link,
    inflow,
    rec_base,
    rec_old,
    dual_base,
    half,
    bars,
    run,
    run_far,
    run_want,
    link_lhs,
    link_img,
    table_col_v,
    table_row_v,
    table_far_v,
    table_want_v,
    chain_v,
    table_col,
    table_row,
    table_far,
    table_want,
    idx_send,
    idx_recv,
    term_send,
    term_recv,
    col_send,
    col_recv,
    z_recv,
    b_recv,
    load_sem,
    idx_sem,
    sems,
):
    me_s = lax.axis_index("scen")
    me_b = lax.axis_index("blk")
    mx, my, mc = me_b // 8, (me_b // 2) % 4, me_b % 2

    def peer(step):
        jx, jy, jc = step
        return (((mx + jx) % 4) * 4 + (my + jy) % 4) * 2 + (mc + jc) % 2

    def source(step):
        return peer(tuple(-d for d in step))

    def taken(step):
        back = tuple(-d % n for d, n in zip(step, (4, 4, 2)))
        return TAKE.index(ORDER.index(back))

    def group_peer(k):
        return (me_s + k // 2) % NS, me_b - mc + (mc + k) % 2

    barrier = pltpu.get_barrier_semaphore()

    def greet(step):
        pl.semaphore_signal(barrier, inc=1, device_id=(me_s, peer(step)), device_id_type=MESH)

    for step in ORDER[:-1]:
        greet(step)

    def greet_z(k, c):
        z, b = group_peer(k)
        pl.semaphore_signal(barrier, inc=1, device_id=(z, b), device_id_type=MESH)
        return c

    lax.fori_loop(2, 2 * NS, greet_z, 0)

    def load(src, dst, i):
        copy = pltpu.make_async_copy(src, dst, load_sem.at[i])
        copy.start()
        return copy

    load_dual = load(dual_h, dual, 5)
    load_far_rows = load(far_rows_h, far_rows_s, 3)
    load_far = load(far_h, far, 6)
    load_rows = load(local_rows_h, local_rows_v, 0)
    load_cols = load(local_cols_h, local_cols_v, 1)
    load_far_cols = load(far_cols_h, far_cols_s, 4)
    load_link_rows = load(link_rows_h, link_rows_s, 7)
    load_link_cols = load(link_cols_h, link_cols_s, 8)
    load_first = load(first_h, first_own, 10)
    load_first_cost = load(first_cost_h, first_own_cost, 11)

    zero = jnp.zeros((S, TILE), F32)
    run[NL] = zero
    run_far[NF] = zero
    run_want[NF] = zero

    load_dual.wait()

    def first_half(rb, c):
        half[rb] = dual[:, pl.ds(pl.multiple_of(rb * TILE, TILE), TILE)].astype(BF16)
        return c

    lax.fori_loop(0, RB, first_half, 0, unroll=8)
    load_far_rows.wait()
    load_far.wait()
    load_link = load(link_h, link, 9)
    load_tiles = load(local_h, tiles, 12)
    load_cost = load(cost_h, cost_v, 13)
    load_rec = load(rec_h, rec, 14)
    load_inflow = load(inflow_h, inflow, 15)

    def send_all(it, src, dst, which):
        def one(i):
            p = peer(ORDER[i])
            group = [i in g for g in GROUPS].index(True)
            pltpu.make_async_remote_copy(
                src_ref=src.at[it, p],
                dst_ref=dst.at[it, me_b],
                send_sem=sems.at[it, which, 3],
                recv_sem=sems.at[it, which, group],
                device_id=(me_s, p),
                device_id_type=MESH,
            ).start()

        return one

    def bytes_of(buffer, count, sem):
        view = buffer.at[pl.ds(0, count)]
        pltpu.make_async_copy(view, view, sem).wait()

    def new_duals(r, last):
        return dual_base[r] - DUAL * (run_far[last] + link_img[pl.ds(r, 1), :])

    def new_recourse(b, last):
        new = jnp.maximum(rec_base[b] + PRIMAL * run_want[last], 0.0)
        return new, (2.0 * new - rec_old[b]).astype(BF16)

    for it in range(ITERS):
        send_term = send_all(it, term_send, term_recv, 0)
        width = NB if it == 0 else 8
        for g in range(0, NB, width):
            for step in ORDER[g : g + width]:
                p = peer(step)
                r = far_rows_s[0, p]
                if it == 0:
                    value = half[r]
                else:
                    value = new_duals(r, table_far[1, r]).astype(BF16)
                term_send[it, p] = dot(value, far[p]).astype(BF16)
            if it == 0:
                load_far_cols.wait()
                for p in range(NB):
                    idx_send[p] = jnp.full((1, TILE), far_cols_s[0, p], jnp.int32)
                pl.semaphore_wait(barrier, NB - 1 + 2 * NS - 2)
                for step in ORDER[:-1]:
                    p = peer(step)
                    pltpu.make_async_remote_copy(
                        src_ref=idx_send.at[p],
                        dst_ref=idx_recv.at[me_b],
                        send_sem=idx_sem.at[0],
                        recv_sem=idx_sem.at[1],
                        device_id=(me_s, p),
                        device_id_type=MESH,
                    ).start()
            for i in range(g, min(g + width, NB - 1)):
                send_term(i)
        term_recv[it, me_b] = term_send[it, me_b]

        if it == 0:
            load_first.wait()
            load_first_cost.wait()
            first_recv[me_s, 0:XB] = first_own[...]
            first_recv[me_s, XB : 2 * XB] = first_own_cost[...]
            first_recv[me_s, 2 * XB :] = jnp.zeros((8 - 2 * XB, TILE), F32)

            def send_first(k, c):
                pltpu.make_async_remote_copy(
                    src_ref=first_recv.at[me_s],
                    dst_ref=first_recv.at[me_s],
                    send_sem=idx_sem.at[2],
                    recv_sem=idx_sem.at[3],
                    device_id=((me_s + k) % NS, me_b),
                    device_id_type=MESH,
                ).start()
                return c

            lax.fori_loop(1, NS, send_first, 0)
            load_link_rows.wait()
            load_link_cols.wait()
            load_link.wait()

        for n in range(NK):
            r = link_rows_s[0, n]
            if it == 0:
                value = half[r]
            else:
                value = new_duals(r, table_far[1, r]).astype(BF16)
            link_lhs[n : n + 1, :] = jnp.sum(value.astype(F32), axis=0, keepdims=True)
        sums = link_lhs[...]
        high = sums.astype(BF16)
        low = (sums - high.astype(F32)).astype(BF16)
        lhs = jnp.concatenate([high, low], axis=0)
        block = lax.broadcasted_iota(jnp.int32, (FB, TILE), 0)
        part = jnp.zeros((FB, TILE), F32)
        for n in range(NK):
            both = dot(lhs, link[n])
            row = both[n : n + 1] + both[NK + n : NK + n + 1]
            part = part + jnp.where(block == link_cols_s[0, n], row, 0.0)
        own = me_s * 2 + mc
        z_recv[it, own] = part.astype(BF16)

        def send_z(k, c):
            z, b = group_peer(k)
            pltpu.make_async_remote_copy(
                src_ref=z_recv.at[it, own],
                dst_ref=z_recv.at[it, own],
                send_sem=sems.at[it, 1, 0],
                recv_sem=sems.at[it, 1, 1],
                device_id=(z, b),
                device_id_type=MESH,
            ).start()
            return c

        lax.fori_loop(1, 2 * NS, send_z, 0)

        def to_half(rb, c):
            new = new_duals(rb, table_far[1, rb])
            dual[:, pl.ds(pl.multiple_of(rb * TILE, TILE), TILE)] = new
            half[rb] = new.astype(BF16)
            return c

        if it > 0:
            lax.fori_loop(0, RB, to_half, 0, unroll=8)

        if it == 0:
            load_rows.wait()
            load_cols.wait()
            pad = jnp.full((8, W - NL), 64.0, F32)
            row_key = jnp.concatenate(
                [jnp.broadcast_to(local_rows_v[...].astype(F32), (8, NL)), pad], axis=1
            )
            col_key = jnp.concatenate(
                [jnp.broadcast_to(local_cols_v[...].astype(F32), (8, NL)), pad], axis=1
            )
            col_tables = sorted_tables(col_key, row_key, NL, W, NL)
            for i, value in enumerate(col_tables):
                table_col_v[i : i + 1, :] = whole(value, COL_LIMITS[i])
            col_to_smem = load(table_col_v, table_col, 0)
            col_to_smem.wait()
            load_tiles.wait()

        def gradient_step(n, total):
            keep = table_col[2, n].astype(F32)
            total = total * keep + dot(half[table_col[1, n]], tiles[table_col[0, n]])
            run[n] = total
            return total

        lax.fori_loop(0, NL, gradient_step, zero, unroll=UNROLL)

        if it == 0:
            load_rec.wait()
            load_cost.wait()

        def base_recourse(cb, c):
            at = pl.ds(pl.multiple_of(cb * TILE, TILE), TILE)
            old = rec[:, at]
            rec_old[cb] = old
            rec_base[cb] = old - PRIMAL * (cost_v[:, at] - run[table_col[3, cb]])
            return c

        lax.fori_loop(0, CB, base_recourse, 0, unroll=8)

        if it == 0:

            def turn(q, c):
                far_t[q] = far[q].T
                return c

            lax.fori_loop(0, NF, turn, 0, unroll=8)

            row_tables = sorted_tables(row_key, col_key, NL, W, NL)
            for i, value in enumerate(row_tables):
                table_row_v[i : i + 1, :] = whole(value, ROW_LIMITS[i])
            row_to_smem = load(table_row_v, table_row, 1)

            lane = lax.broadcasted_iota(jnp.int32, (1, WF), 1)
            key = jnp.full((1, WF), 64, jnp.int32)
            for k, i in enumerate(TAKE):
                row = jnp.full((1, WF), far_rows_s[0, source(ORDER[i])], jnp.int32)
                chain_v[k : k + 1, :] = row
                key = jnp.where(lane == k, row, key)
            for i, value in enumerate(chain_tables(chain_v[...], key)):
                table_far_v[i : i + 1, :] = value
            far_to_smem = load(table_far_v, table_far, 2)

            bytes_of(idx_recv, NB - 1, idx_sem.at[1])
            idx_recv[me_b] = idx_send[me_b]
            key = jnp.full((1, WF), 64, jnp.int32)
            for k, i in enumerate(TAKE):
                row = idx_recv[source(ORDER[i])]
                chain_v[k : k + 1, :] = row
                key = jnp.where(lane == k, row, key)
            for i, value in enumerate(chain_tables(chain_v[...], key)):
                table_want_v[i : i + 1, :] = value
            table_want_v[2:3, :] = jnp.minimum(key, CB - 1)
            want_to_smem = load(table_want_v, table_want, 0)

        bytes_of(z_recv.at[it], 2 * NS - 1, sems.at[it, 1, 1])
        total = z_recv[it, 0].astype(F32)
        for k in range(1, 2 * NS):
            total = total + z_recv[it, k].astype(F32)
        place = me_b // 2
        b_recv[it, place] = total.astype(BF16)
        for step in STEPS[:-1]:
            pltpu.make_async_remote_copy(
                src_ref=b_recv.at[it, place],
                dst_ref=b_recv.at[it, place],
                send_sem=sems.at[it, 3, 0],
                recv_sem=sems.at[it, 3, 1],
                device_id=(me_s, peer(step + (0,))),
                device_id_type=MESH,
            ).start()

        if it == 0:
            want_to_smem.wait()
        for k, i in enumerate(TAKE):
            for j, g in enumerate(GROUPS):
                if i == g[0]:
                    bytes_of(term_recv.at[it], len(g), sems.at[it, 0, j])
            term = term_recv[it, source(ORDER[i])].astype(F32)
            run_want[k] = run_want[table_want[0, k]] + term

        send_col = send_all(it, col_send, col_recv, 2)
        for g in range(0, NB, 8):
            for step in ORDER[g : g + 8]:
                p = peer(step)
                w = table_want[2, taken(step)]
                col_send[it, p] = new_recourse(w, table_want[1, w])[1]
            for i in range(g, min(g + 8, NB - 1)):
                send_col(i)
        col_recv[it, me_b] = col_send[it, me_b]

        def update_recourse(cb, c):
            new, bar = new_recourse(cb, table_want[1, cb])
            bars[cb] = bar
            rec[:, pl.ds(pl.multiple_of(cb * TILE, TILE), TILE)] = new
            return c

        lax.fori_loop(0, CB, update_recourse, 0, unroll=8)

        if it == 0:
            row_to_smem.wait()
            far_to_smem.wait()
        def image_step(n, total):
            keep = table_row[2, n].astype(F32)
            if it == 0:
                tile = tiles[table_row[0, n]].T
                tiles_t[n] = tile
            else:
                tile = tiles_t[n]
            total = total * keep + dot(bars[table_row[1, n]], tile)
            run[n] = total
            return total

        lax.fori_loop(0, NL, image_step, zero, unroll=UNROLL)
        if it == 0:
            load_inflow.wait()

        def base_duals(rb, c):
            at = pl.ds(pl.multiple_of(rb * TILE, TILE), TILE)
            dual_base[rb] = dual[:, at] + DUAL * (
                inflow[:, at].astype(F32) - run[table_row[3, rb]]
            )
            return c

        lax.fori_loop(0, RB, base_duals, 0, unroll=8)

        if it == 0:
            bytes_of(first_recv, NS - 1, idx_sem.at[3])
            for s in range(NS):
                first_full[s * XB : (s + 1) * XB, :] = first_recv[s, 0:XB]
                first_cost[s * XB : (s + 1) * XB, :] = first_recv[s, XB : 2 * XB]
        bytes_of(b_recv.at[it], NB // 2 - 1, sems.at[it, 3, 1])
        total = b_recv[it, 0].astype(F32)
        for k in range(1, NB // 2):
            total = total + b_recv[it, k].astype(F32)
        old_first = first_full[...]
        new_first = jnp.maximum(
            old_first - FIRST * (first_cost[...] - total / (S * NS)), 0.0
        )
        first_full[...] = new_first
        if it == ITERS - 1:
            for i in range(XB):
                first_out[i : i + 1, :] = first_full[pl.ds(me_s * XB + i, 1), :]

        link_img[0:FB, :] = 2.0 * new_first - old_first
        for n in range(NK):
            link_lhs[n : n + 1, :] = link_img[pl.ds(link_cols_s[0, n], 1), :]
        lhs = link_lhs[...].astype(BF16)
        block = lax.broadcasted_iota(jnp.int32, (RB, TILE), 0)
        image = jnp.zeros((RB, TILE), F32)
        for n in range(NK):
            row = dot_t(lhs, link[n])[n : n + 1]
            image = image + jnp.where(block == link_rows_s[0, n], row, 0.0)
        link_img[...] = image

        for k, i in enumerate(TAKE):
            for j, g in enumerate(GROUPS):
                if i == g[0]:
                    bytes_of(col_recv.at[it], len(g), sems.at[it, 2, j])
            q = source(ORDER[i])
            run_far[k] = run_far[table_far[0, k]] + dot(col_recv[it, q], far_t[q])

    def update_duals(rb, c):
        at = pl.ds(pl.multiple_of(rb * TILE, TILE), TILE)
        dual[:, at] = new_duals(rb, table_far[1, rb])
        return c

    lax.fori_loop(0, RB, update_duals, 0, unroll=10)
    bytes_of(idx_recv, NB - 1, idx_sem.at[0])
    bytes_of(first_recv, NS - 1, idx_sem.at[2])
    for it in range(ITERS):
        bytes_of(term_recv.at[it], NB - 1, sems.at[it, 0, 3])
        bytes_of(z_recv.at[it], 2 * NS - 1, sems.at[it, 1, 0])
        bytes_of(col_recv.at[it], NB - 1, sems.at[it, 2, 3])
        bytes_of(b_recv.at[it], NB // 2 - 1, sems.at[it, 3, 0])


def hand_out(first, rec, dual, first_out, rec_out, dual_out, sem):
    copies = [
        pltpu.make_async_copy(first, first_out, sem.at[0]),
        pltpu.make_async_copy(rec, rec_out, sem.at[1]),
        pltpu.make_async_copy(dual, dual_out, sem.at[2]),
    ]
    for copy in copies:
        copy.start()
    for copy in copies:
        copy.wait()


def body(
    local_tiles,
    local_rows,
    local_cols,
    far_tiles,
    far_rows,
    far_cols,
    link_tiles,
    link_rows,
    link_cols,
    inflows,
    recourse_cost,
    first_cost,
    first_section,
    recourse,
    duals,
):
    hbm = pl.BlockSpec(memory_space=pltpu.HBM)
    dma = pltpu.SemaphoreType.DMA
    vmem, smem = pltpu.VMEM, pltpu.SMEM
    int32 = jnp.int32
    shapes = (
        jax.ShapeDtypeStruct((XB, TILE), F32),
        jax.ShapeDtypeStruct((S, CB * TILE), F32),
        jax.ShapeDtypeStruct((S, RB * TILE), F32),
    )
    held = [vmem(shape.shape, F32) for shape in shapes]
    results = pl.pallas_call(
        kernel,
        out_shape=held,
        in_specs=[hbm] * 15,
        out_specs=[pl.BlockSpec(memory_space=vmem)] * 3,
        scratch_shapes=[
            smem((1, NF), int32),
            smem((1, NF), int32),
            smem((1, NK), int32),
            smem((1, NK), int32),
            vmem((1, NL), int32),
            vmem((1, NL), int32),
            vmem((1, CB * TILE), F32),
            vmem((XB, TILE), F32),
            vmem((XB, TILE), F32),
            vmem((NS, 8, TILE), F32),
            vmem((FB, TILE), F32),
            vmem((FB, TILE), F32),
            vmem((NL, TILE, TILE), BF16),
            vmem((NL, TILE, TILE), BF16),
            vmem((NF, TILE, TILE), BF16),
            vmem((NF, TILE, TILE), BF16),
            vmem((NK, TILE, TILE), BF16),
            vmem((S, RB * TILE), BF16),
            vmem((CB, S, TILE), F32),
            vmem((CB, S, TILE), F32),
            vmem((RB, S, TILE), F32),
            vmem((RB, S, TILE), BF16),
            vmem((CB, S, TILE), BF16),
            vmem((NL + 1, S, TILE), F32),
            vmem((NF + 1, S, TILE), F32),
            vmem((NF + 1, S, TILE), F32),
            vmem((NK, TILE), F32),
            vmem((RB, TILE), F32),
            vmem((4, W), int32),
            vmem((4, W), int32),
            vmem((2, WF), int32),
            vmem((3, WF), int32),
            vmem((NF, WF), int32),
            smem((4, W), int32),
            smem((4, W), int32),
            smem((2, WF), int32),
            smem((3, WF), int32),
            vmem((NB, 1, TILE), int32),
            vmem((NB, 1, TILE), int32),
            vmem((ITERS, NB, S, TILE), BF16),
            vmem((ITERS, NB, S, TILE), BF16),
            vmem((ITERS, NB, S, TILE), BF16),
            vmem((ITERS, NB, S, TILE), BF16),
            vmem((ITERS, 2 * NS, FB, TILE), BF16),
            vmem((ITERS, NB // 2, FB, TILE), BF16),
            dma((16,)),
            dma((4,)),
            dma((ITERS, 4, 4)),
        ],
        compiler_params=pltpu.CompilerParams(
            collective_id=0, has_side_effects=True, vmem_limit_bytes=60 << 20
        ),
        name="dispatch",
    )(
        far_rows.reshape(1, NF),
        far_cols.reshape(1, NF),
        link_rows.reshape(1, NK),
        link_cols.reshape(1, NK),
        local_rows.reshape(1, NL),
        local_cols.reshape(1, NL),
        recourse_cost.reshape(1, CB * TILE),
        first_cost.reshape(XB, TILE),
        first_section.reshape(XB, TILE),
        local_tiles,
        far_tiles.reshape(NF, TILE, TILE),
        link_tiles,
        inflows,
        recourse,
        duals,
    )
    first_out, rec_out, dual_out = pl.pallas_call(
        hand_out,
        out_shape=shapes,
        in_specs=[pl.BlockSpec(memory_space=vmem)] * 3,
        out_specs=(hbm, hbm, hbm),
        scratch_shapes=[dma((3,))],
        compiler_params=pltpu.CompilerParams(vmem_limit_bytes=60 << 20),
        name="hand_out",
    )(*(pltpu.with_memory_space_constraint(result, vmem) for result in results))
    return first_out.reshape(XB * TILE), rec_out, dual_out


def solution(mesh):
    in_specs = (
        P("blk", None, None),
        P("blk"),
        P("blk"),
        P("blk", None, None, None),
        P("blk", None),
        P("blk", None),
        P(("scen", "blk"), None, None),
        P(("scen", "blk")),
        P(("scen", "blk")),
        P("scen", "blk"),
        P("blk"),
        P("scen"),
        P("scen"),
        P("scen", "blk"),
        P("scen", "blk"),
    )
    out_specs = (P("scen"), P("scen", "blk"), P("scen", "blk"))
    return jax.shard_map(body, mesh=mesh, in_specs=in_specs, out_specs=out_specs, check_vma=False)
```

```python
import functools

import jax
import jax.numpy as jnp
from jax import lax
from jax.experimental import pallas as pl
from jax.experimental.pallas import tpu as pltpu
from jax.sharding import PartitionSpec as P

TILE = 128
ITERS = 2
S = 32
RB = 40
CB = 32
NL = 224
NF = 32
NK = 16
XB = 2
NS = 8
NB = 32
FB = XB * NS
W = 256
WF = 128
STEPS = sorted(
    ((a, b) for a in range(4) for b in range(4)),
    key=lambda d: -(min(d[0], 4 - d[0]) + min(d[1], 4 - d[1])),
)
ORDER = [(a, b, c) for c in (1, 0) for a, b in STEPS]
GROUPS = tuple(
    tuple(i for i in range(NB - 1) if i % 16 in part)
    for part in (range(0, 5), range(5, 11), range(11, 16))
)
TAKE = [NB - 1] + [i for part in GROUPS[::-1] for i in part]
UNROLL = 56

PRIMAL = 0.4
FIRST = 2.0
DUAL = 0.4
COL_LIMITS = (NL - 1, RB - 1, 1, NL)
ROW_LIMITS = (NL - 1, CB - 1, 1, NL)
MESH = pl.DeviceIdType.MESH
F32 = jnp.float32
BF16 = jnp.bfloat16


def dot(a, b):
    return jnp.dot(a, b, preferred_element_type=F32)


def dot_t(a, b):
    return lax.dot_general(a, b, (((1,), (1,)), ((), ())), preferred_element_type=F32)


def whole(value, top):
    return jnp.clip(value[0:1].astype(jnp.int32), 0, top)


def chain_tables(column, key):
    rows = lax.broadcasted_iota(jnp.int32, (NF, WF), 0)
    lanes = lax.broadcasted_iota(jnp.int32, (NF, WF), 1)
    result = []
    for hit in ((column == key) & (rows < lanes), column == lanes):
        top = jnp.max(jnp.where(hit, rows + 1, 0), axis=0, keepdims=True)
        result.append(jnp.where(top == 0, NF, top - 1))
    return result


def sorted_tables(key, other, count, width, empty):
    rows = lax.broadcasted_iota(jnp.int32, (width, width), 0).astype(F32)
    lanes = lax.broadcasted_iota(jnp.int32, (width, width), 1).astype(F32)
    key_j = jnp.broadcast_to(key[0:1], (width, width))
    key_i = key_j.T
    before = (key_j * W + lanes) < (key_i * W + rows)
    rank = dot(before.astype(F32).astype(BF16), jnp.ones((width, width), BF16))
    place = (rank == lanes).astype(F32).astype(BF16)
    lane8 = lax.broadcasted_iota(jnp.int32, (8, width), 1).astype(F32)
    source = jnp.concatenate([lane8, other, key, key], axis=0).astype(BF16)
    moved = dot(source, place)
    order, other_sorted, key_sorted = moved[0:8], moved[8:16], moved[16:24]
    previous = pltpu.roll(key_sorted, 1, 1)
    keep = ((key_sorted == previous) & (lane8 > 0)).astype(F32)
    ones = jnp.ones((16, width), BF16)
    under = dot(ones, (key_i < lanes).astype(F32).astype(BF16))[0:8]
    upto = pltpu.roll(under, width - 1, 1)
    last = jnp.where(upto > under, upto - 1.0, float(empty))
    return order, other_sorted, keep, last


def kernel(
    far_rows_h,
    far_cols_h,
    link_rows_h,
    link_cols_h,
    local_rows_h,
    local_cols_h,
    cost_h,
    first_cost_h,
    first_h,
    local_h,
    far_h,
    link_h,
    inflow_h,
    rec_h,
    dual_h,
    first_out,
    rec,
    dual,
    far_rows_s,
    far_cols_s,
    link_rows_s,
    link_cols_s,
    local_rows_v,
    local_cols_v,
    cost_v,
    first_own,
    first_own_cost,
    first_recv,
    first_full,
    first_cost,
    tiles,
    tiles_t,
    far,
    far_t,
    link,
    inflow,
    rec_base,
    rec_old,
    dual_base,
    half,
    bars,
    run,
    run_far,
    run_want,
    link_lhs,
    link_img,
    table_col_v,
    table_row_v,
    table_far_v,
    table_want_v,
    chain_v,
    table_col,
    table_row,
    table_far,
    table_want,
    idx_send,
    idx_recv,
    term_send,
    term_recv,
    col_send,
    col_recv,
    z_recv,
    b_recv,
    load_sem,
    idx_sem,
    sems,
):
    me_s = lax.axis_index("scen")
    me_b = lax.axis_index("blk")
    mx, my, mc = me_b // 8, (me_b // 2) % 4, me_b % 2

    def peer(step):
        jx, jy, jc = step
        return (((mx + jx) % 4) * 4 + (my + jy) % 4) * 2 + (mc + jc) % 2

    def source(step):
        return peer(tuple(-d for d in step))

    def taken(step):
        back = tuple(-d % n for d, n in zip(step, (4, 4, 2)))
        return TAKE.index(ORDER.index(back))

    def group_peer(k):
        return (me_s + k // 2) % NS, me_b - mc + (mc + k) % 2

    barrier = pltpu.get_barrier_semaphore()

    def greet(step):
        pl.semaphore_signal(barrier, inc=1, device_id=(me_s, peer(step)), device_id_type=MESH)

    def greet_z(k):
        z, b = group_peer(k)
        pl.semaphore_signal(barrier, inc=1, device_id=(z, b), device_id_type=MESH)

    for k in sorted(range(2, 2 * NS), key=lambda k: -min(k // 2, NS - k // 2)):
        greet_z(k)

    for step in ORDER[:-1]:
        greet(step)

    def load(src, dst, i):
        copy = pltpu.make_async_copy(src, dst, load_sem.at[i])
        copy.start()
        return copy

    load_dual = load(dual_h, dual, 5)
    load_far_rows = load(far_rows_h, far_rows_s, 3)
    load_far = load(far_h, far, 6)
    load_rows = load(local_rows_h, local_rows_v, 0)
    load_cols = load(local_cols_h, local_cols_v, 1)
    load_far_cols = load(far_cols_h, far_cols_s, 4)
    load_link_rows = load(link_rows_h, link_rows_s, 7)
    load_link_cols = load(link_cols_h, link_cols_s, 8)
    load_first = load(first_h, first_own, 10)
    load_first_cost = load(first_cost_h, first_own_cost, 11)

    zero = jnp.zeros((S, TILE), F32)
    run[NL] = zero
    run_far[NF] = zero
    run_want[NF] = zero

    load_dual.wait()

    def first_half(rb, c):
        half[rb] = dual[:, pl.ds(pl.multiple_of(rb * TILE, TILE), TILE)].astype(BF16)
        return c

    lax.fori_loop(0, RB, first_half, 0, unroll=8)
    load_far_rows.wait()
    load_far.wait()
    load_link = load(link_h, link, 9)
    load_tiles = load(local_h, tiles, 12)
    load_cost = load(cost_h, cost_v, 13)
    load_rec = load(rec_h, rec, 14)
    load_inflow = load(inflow_h, inflow, 15)

    def send_all(it, src, dst, which):
        def one(i):
            p = peer(ORDER[i])
            group = [i in g for g in GROUPS].index(True)
            pltpu.make_async_remote_copy(
                src_ref=src.at[it, p],
                dst_ref=dst.at[it, me_b],
                send_sem=sems.at[it, which, 3],
                recv_sem=sems.at[it, which, group],
                device_id=(me_s, p),
                device_id_type=MESH,
            ).start()

        return one

    def bytes_of(buffer, count, sem):
        view = buffer.at[pl.ds(0, count)]
        pltpu.make_async_copy(view, view, sem).wait()

    def new_duals(r, last):
        return dual_base[r] - DUAL * (run_far[last] + link_img[pl.ds(r, 1), :])

    def new_recourse(b, last):
        new = jnp.maximum(rec_base[b] + PRIMAL * run_want[last], 0.0)
        return new, (2.0 * new - rec_old[b]).astype(BF16)

    for it in range(ITERS):
        send_term = send_all(it, term_send, term_recv, 0)
        width = NB if it == 0 else 8
        for g in range(0, NB, width):
            for step in ORDER[g : g + width]:
                p = peer(step)
                r = far_rows_s[0, p]
                if it == 0:
                    value = half[r]
                else:
                    value = new_duals(r, table_far[1, r]).astype(BF16)
                term_send[it, p] = dot(value, far[p]).astype(BF16)
            if it == 0:
                load_far_cols.wait()
                for p in range(NB):
                    idx_send[p] = jnp.full((1, TILE), far_cols_s[0, p], jnp.int32)
                pl.semaphore_wait(barrier, NB - 1 + 2 * NS - 2)
                for step in ORDER[:-1]:
                    p = peer(step)
                    pltpu.make_async_remote_copy(
                        src_ref=idx_send.at[p],
                        dst_ref=idx_recv.at[me_b],
                        send_sem=idx_sem.at[0],
                        recv_sem=idx_sem.at[1],
                        device_id=(me_s, p),
                        device_id_type=MESH,
                    ).start()
            for i in range(g, min(g + width, NB - 1)):
                send_term(i)
        term_recv[it, me_b] = term_send[it, me_b]

        if it == 0:
            load_first.wait()
            load_first_cost.wait()
            first_recv[me_s, 0:XB] = first_own[...]
            first_recv[me_s, XB : 2 * XB] = first_own_cost[...]
            first_recv[me_s, 2 * XB :] = jnp.zeros((8 - 2 * XB, TILE), F32)

            def send_first(k, c):
                pltpu.make_async_remote_copy(
                    src_ref=first_recv.at[me_s],
                    dst_ref=first_recv.at[me_s],
                    send_sem=idx_sem.at[2],
                    recv_sem=idx_sem.at[3],
                    device_id=((me_s + k) % NS, me_b),
                    device_id_type=MESH,
                ).start()
                return c

            lax.fori_loop(1, NS, send_first, 0)
            load_link_rows.wait()
            load_link_cols.wait()
            load_link.wait()

        for n in range(NK):
            r = link_rows_s[0, n]
            if it == 0:
                value = half[r]
            else:
                value = new_duals(r, table_far[1, r]).astype(BF16)
            link_lhs[n : n + 1, :] = jnp.sum(value.astype(F32), axis=0, keepdims=True)
        sums = link_lhs[...]
        high = sums.astype(BF16)
        low = (sums - high.astype(F32)).astype(BF16)
        lhs = jnp.concatenate([high, low], axis=0)
        block = lax.broadcasted_iota(jnp.int32, (FB, TILE), 0)
        part = jnp.zeros((FB, TILE), F32)
        for n in range(NK):
            both = dot(lhs, link[n])
            row = both[n : n + 1] + both[NK + n : NK + n + 1]
            part = part + jnp.where(block == link_cols_s[0, n], row, 0.0)
        own = me_s * 2 + mc
        z_recv[it, own] = part.astype(BF16)

        def send_z(k):
            z, b = group_peer(k)
            pltpu.make_async_remote_copy(
                src_ref=z_recv.at[it, own],
                dst_ref=z_recv.at[it, own],
                send_sem=sems.at[it, 1, 0],
                recv_sem=sems.at[it, 1, 1],
                device_id=(z, b),
                device_id_type=MESH,
            ).start()

        for k in sorted(range(1, 2 * NS), key=lambda k: -min(k // 2, NS - k // 2)):
            send_z(k)

        def to_half(rb, c):
            new = new_duals(rb, table_far[1, rb])
            dual[:, pl.ds(pl.multiple_of(rb * TILE, TILE), TILE)] = new
            half[rb] = new.astype(BF16)
            return c

        if it > 0:
            lax.fori_loop(0, RB, to_half, 0, unroll=8)

        if it == 0:
            load_rows.wait()
            load_cols.wait()
            pad = jnp.full((8, W - NL), 64.0, F32)
            row_key = jnp.concatenate(
                [jnp.broadcast_to(local_rows_v[...].astype(F32), (8, NL)), pad], axis=1
            )
            col_key = jnp.concatenate(
                [jnp.broadcast_to(local_cols_v[...].astype(F32), (8, NL)), pad], axis=1
            )
            col_tables = sorted_tables(col_key, row_key, NL, W, NL)
            for i, value in enumerate(col_tables):
                table_col_v[i : i + 1, :] = whole(value, COL_LIMITS[i])
            col_to_smem = load(table_col_v, table_col, 0)
            col_to_smem.wait()
            load_tiles.wait()

        def gradient_step(n, total):
            keep = table_col[2, n].astype(F32)
            total = total * keep + dot(half[table_col[1, n]], tiles[table_col[0, n]])
            run[n] = total
            return total

        lax.fori_loop(0, NL, gradient_step, zero, unroll=UNROLL)

        if it == 0:
            load_rec.wait()
            load_cost.wait()

        def base_recourse(cb, c):
            at = pl.ds(pl.multiple_of(cb * TILE, TILE), TILE)
            old = rec[:, at]
            rec_old[cb] = old
            rec_base[cb] = old - PRIMAL * (cost_v[:, at] - run[table_col[3, cb]])
            return c

        lax.fori_loop(0, CB, base_recourse, 0, unroll=8)

        if it == 0:

            def turn(q, c):
                far_t[q] = far[q].T
                return c

            lax.fori_loop(0, NF, turn, 0, unroll=8)

            row_tables = sorted_tables(row_key, col_key, NL, W, NL)
            for i, value in enumerate(row_tables):
                table_row_v[i : i + 1, :] = whole(value, ROW_LIMITS[i])
            row_to_smem = load(table_row_v, table_row, 1)

            lane = lax.broadcasted_iota(jnp.int32, (1, WF), 1)
            key = jnp.full((1, WF), 64, jnp.int32)
            for k, i in enumerate(TAKE):
                row = jnp.full((1, WF), far_rows_s[0, source(ORDER[i])], jnp.int32)
                chain_v[k : k + 1, :] = row
                key = jnp.where(lane == k, row, key)
            for i, value in enumerate(chain_tables(chain_v[...], key)):
                table_far_v[i : i + 1, :] = value
            far_to_smem = load(table_far_v, table_far, 2)

            bytes_of(idx_recv, NB - 1, idx_sem.at[1])
            idx_recv[me_b] = idx_send[me_b]
            key = jnp.full((1, WF), 64, jnp.int32)
            for k, i in enumerate(TAKE):
                row = idx_recv[source(ORDER[i])]
                chain_v[k : k + 1, :] = row
                key = jnp.where(lane == k, row, key)
            for i, value in enumerate(chain_tables(chain_v[...], key)):
                table_want_v[i : i + 1, :] = value
            table_want_v[2:3, :] = jnp.minimum(key, CB - 1)
            want_to_smem = load(table_want_v, table_want, 0)

        bytes_of(z_recv.at[it], 2 * NS - 1, sems.at[it, 1, 1])
        total = z_recv[it, 0].astype(F32)
        for k in range(1, 2 * NS):
            total = total + z_recv[it, k].astype(F32)
        place = me_b // 2
        b_recv[it, place] = total.astype(BF16)
        for step in STEPS[:-1]:
            pltpu.make_async_remote_copy(
                src_ref=b_recv.at[it, place],
                dst_ref=b_recv.at[it, place],
                send_sem=sems.at[it, 3, 0],
                recv_sem=sems.at[it, 3, 1],
                device_id=(me_s, peer(step + (0,))),
                device_id_type=MESH,
            ).start()

        if it == 0:
            want_to_smem.wait()
        for k, i in enumerate(TAKE):
            for j, g in enumerate(GROUPS):
                if i == g[0]:
                    bytes_of(term_recv.at[it], len(g), sems.at[it, 0, j])
            term = term_recv[it, source(ORDER[i])].astype(F32)
            run_want[k] = run_want[table_want[0, k]] + term

        send_col = send_all(it, col_send, col_recv, 2)
        for g in range(0, NB, 8):
            for step in ORDER[g : g + 8]:
                p = peer(step)
                w = table_want[2, taken(step)]
                col_send[it, p] = new_recourse(w, table_want[1, w])[1]
            for i in range(g, min(g + 8, NB - 1)):
                send_col(i)
        col_recv[it, me_b] = col_send[it, me_b]

        def update_recourse(cb, c):
            new, bar = new_recourse(cb, table_want[1, cb])
            bars[cb] = bar
            rec[:, pl.ds(pl.multiple_of(cb * TILE, TILE), TILE)] = new
            return c

        lax.fori_loop(0, CB, update_recourse, 0, unroll=8)

        if it == 0:
            row_to_smem.wait()
            far_to_smem.wait()
        def image_step(n, total):
            keep = table_row[2, n].astype(F32)
            if it == 0:
                tile = tiles[table_row[0, n]].T
                tiles_t[n] = tile
            else:
                tile = tiles_t[n]
            total = total * keep + dot(bars[table_row[1, n]], tile)
            run[n] = total
            return total

        lax.fori_loop(0, NL, image_step, zero, unroll=UNROLL)
        if it == 0:
            load_inflow.wait()

        def base_duals(rb, c):
            at = pl.ds(pl.multiple_of(rb * TILE, TILE), TILE)
            dual_base[rb] = dual[:, at] + DUAL * (
                inflow[:, at].astype(F32) - run[table_row[3, rb]]
            )
            return c

        lax.fori_loop(0, RB, base_duals, 0, unroll=8)

        if it == 0:
            bytes_of(first_recv, NS - 1, idx_sem.at[3])
            for s in range(NS):
                first_full[s * XB : (s + 1) * XB, :] = first_recv[s, 0:XB]
                first_cost[s * XB : (s + 1) * XB, :] = first_recv[s, XB : 2 * XB]
        bytes_of(b_recv.at[it], NB // 2 - 1, sems.at[it, 3, 1])
        total = b_recv[it, 0].astype(F32)
        for k in range(1, NB // 2):
            total = total + b_recv[it, k].astype(F32)
        old_first = first_full[...]
        new_first = jnp.maximum(
            old_first - FIRST * (first_cost[...] - total / (S * NS)), 0.0
        )
        first_full[...] = new_first
        if it == ITERS - 1:
            for i in range(XB):
                first_out[i : i + 1, :] = first_full[pl.ds(me_s * XB + i, 1), :]

        link_img[0:FB, :] = 2.0 * new_first - old_first
        for n in range(NK):
            link_lhs[n : n + 1, :] = link_img[pl.ds(link_cols_s[0, n], 1), :]
        lhs = link_lhs[...].astype(BF16)
        block = lax.broadcasted_iota(jnp.int32, (RB, TILE), 0)
        image = jnp.zeros((RB, TILE), F32)
        for n in range(NK):
            row = dot_t(lhs, link[n])[n : n + 1]
            image = image + jnp.where(block == link_rows_s[0, n], row, 0.0)
        link_img[...] = image

        for k, i in enumerate(TAKE):
            for j, g in enumerate(GROUPS):
                if i == g[0]:
                    bytes_of(col_recv.at[it], len(g), sems.at[it, 2, j])
            q = source(ORDER[i])
            run_far[k] = run_far[table_far[0, k]] + dot(col_recv[it, q], far_t[q])

    def update_duals(rb, c):
        at = pl.ds(pl.multiple_of(rb * TILE, TILE), TILE)
        dual[:, at] = new_duals(rb, table_far[1, rb])
        return c

    lax.fori_loop(0, RB, update_duals, 0, unroll=10)
    bytes_of(idx_recv, NB - 1, idx_sem.at[0])
    bytes_of(first_recv, NS - 1, idx_sem.at[2])
    for it in range(ITERS):
        bytes_of(term_recv.at[it], NB - 1, sems.at[it, 0, 3])
        bytes_of(z_recv.at[it], 2 * NS - 1, sems.at[it, 1, 0])
        bytes_of(col_recv.at[it], NB - 1, sems.at[it, 2, 3])
        bytes_of(b_recv.at[it], NB // 2 - 1, sems.at[it, 3, 0])


def hand_out(first, rec, dual, first_out, rec_out, dual_out, sem):
    copies = [
        pltpu.make_async_copy(first, first_out, sem.at[0]),
        pltpu.make_async_copy(rec, rec_out, sem.at[1]),
        pltpu.make_async_copy(dual, dual_out, sem.at[2]),
    ]
    for copy in copies:
        copy.start()
    for copy in copies:
        copy.wait()


def body(
    local_tiles,
    local_rows,
    local_cols,
    far_tiles,
    far_rows,
    far_cols,
    link_tiles,
    link_rows,
    link_cols,
    inflows,
    recourse_cost,
    first_cost,
    first_section,
    recourse,
    duals,
):
    hbm = pl.BlockSpec(memory_space=pltpu.HBM)
    dma = pltpu.SemaphoreType.DMA
    vmem, smem = pltpu.VMEM, pltpu.SMEM
    int32 = jnp.int32
    shapes = (
        jax.ShapeDtypeStruct((XB, TILE), F32),
        jax.ShapeDtypeStruct((S, CB * TILE), F32),
        jax.ShapeDtypeStruct((S, RB * TILE), F32),
    )
    held = [vmem(shape.shape, F32) for shape in shapes]
    results = pl.pallas_call(
        kernel,
        out_shape=held,
        in_specs=[hbm] * 15,
        out_specs=[pl.BlockSpec(memory_space=vmem)] * 3,
        scratch_shapes=[
            smem((1, NF), int32),
            smem((1, NF), int32),
            smem((1, NK), int32),
            smem((1, NK), int32),
            vmem((1, NL), int32),
            vmem((1, NL), int32),
            vmem((1, CB * TILE), F32),
            vmem((XB, TILE), F32),
            vmem((XB, TILE), F32),
            vmem((NS, 8, TILE), F32),
            vmem((FB, TILE), F32),
            vmem((FB, TILE), F32),
            vmem((NL, TILE, TILE), BF16),
            vmem((NL, TILE, TILE), BF16),
            vmem((NF, TILE, TILE), BF16),
            vmem((NF, TILE, TILE), BF16),
            vmem((NK, TILE, TILE), BF16),
            vmem((S, RB * TILE), BF16),
            vmem((CB, S, TILE), F32),
            vmem((CB, S, TILE), F32),
            vmem((RB, S, TILE), F32),
            vmem((RB, S, TILE), BF16),
            vmem((CB, S, TILE), BF16),
            vmem((NL + 1, S, TILE), F32),
            vmem((NF + 1, S, TILE), F32),
            vmem((NF + 1, S, TILE), F32),
            vmem((NK, TILE), F32),
            vmem((RB, TILE), F32),
            vmem((4, W), int32),
            vmem((4, W), int32),
            vmem((2, WF), int32),
            vmem((3, WF), int32),
            vmem((NF, WF), int32),
            smem((4, W), int32),
            smem((4, W), int32),
            smem((2, WF), int32),
            smem((3, WF), int32),
            vmem((NB, 1, TILE), int32),
            vmem((NB, 1, TILE), int32),
            vmem((ITERS, NB, S, TILE), BF16),
            vmem((ITERS, NB, S, TILE), BF16),
            vmem((ITERS, NB, S, TILE), BF16),
            vmem((ITERS, NB, S, TILE), BF16),
            vmem((ITERS, 2 * NS, FB, TILE), BF16),
            vmem((ITERS, NB // 2, FB, TILE), BF16),
            dma((16,)),
            dma((4,)),
            dma((ITERS, 4, 4)),
        ],
        compiler_params=pltpu.CompilerParams(
            collective_id=0, has_side_effects=True, vmem_limit_bytes=60 << 20
        ),
        name="dispatch",
    )(
        far_rows.reshape(1, NF),
        far_cols.reshape(1, NF),
        link_rows.reshape(1, NK),
        link_cols.reshape(1, NK),
        local_rows.reshape(1, NL),
        local_cols.reshape(1, NL),
        recourse_cost.reshape(1, CB * TILE),
        first_cost.reshape(XB, TILE),
        first_section.reshape(XB, TILE),
        local_tiles,
        far_tiles.reshape(NF, TILE, TILE),
        link_tiles,
        inflows,
        recourse,
        duals,
    )
    first_out, rec_out, dual_out = pl.pallas_call(
        hand_out,
        out_shape=shapes,
        in_specs=[pl.BlockSpec(memory_space=vmem)] * 3,
        out_specs=(hbm, hbm, hbm),
        scratch_shapes=[dma((3,))],
        compiler_params=pltpu.CompilerParams(vmem_limit_bytes=60 << 20),
        name="hand_out",
    )(*(pltpu.with_memory_space_constraint(result, vmem) for result in results))
    return first_out.reshape(XB * TILE), rec_out, dual_out


def solution(mesh):
    in_specs = (
        P("blk", None, None),
        P("blk"),
        P("blk"),
        P("blk", None, None, None),
        P("blk", None),
        P("blk", None),
        P(("scen", "blk"), None, None),
        P(("scen", "blk")),
        P(("scen", "blk")),
        P("scen", "blk"),
        P("blk"),
        P("scen"),
        P("scen"),
        P("scen", "blk"),
        P("scen", "blk"),
    )
    out_specs = (P("scen"), P("scen", "blk"), P("scen", "blk"))
    return jax.shard_map(body, mesh=mesh, in_specs=in_specs, out_specs=out_specs, check_vma=False)
```
